128 devices in a mesh: row: 16 (over x, y_lo, core), col: 8 (over z, y_hi).
Axes of the slice: x: 4, y: 4 (y_hi: 2, y_lo: 2; y = y_hi * 2 + y_lo), z: 4, core: 2. Of those that a mesh axis runs over, the one named last changes fastest.
Arguments:
- inputs: bfloat16 [768, 12288], P('row', 'col'), may hold values from -6 to 6
- first_values: bfloat16 [96, 96, 128, 128], P('col', 'row'), may hold values from -0.109375 to 0.109375
- first_blocks: int32 [96, 96], P('col', 'row'), may hold values from 0 to 383, as said below
- second_values: bfloat16 [384, 24, 128, 128], P('row', 'col'), may hold values from -0.0546875 to 0.0546875
- second_blocks: int32 [384, 24], P('row', 'col'), may hold values from 0 to 95, as said below
- cotangent: bfloat16 [768, 12288], P('row', 'col'), may hold values from -6 to 6
Outputs:
- outputs: bfloat16 [768, 12288], P('row', 'col')
- input_grad: bfloat16 [768, 12288], P('row', 'col')
- first_grad: bfloat16 [96, 96, 128, 128], P('col', 'row')
- second_grad: bfloat16 [384, 24, 128, 128], P('row', 'col')
The draws below stay inside these ranges and needn't reach their ends.
Inputs may be any that keep to these rules, and one draw needn't show every extreme that they name: `first_blocks`: in block row i, slots g * 6 to (g + 1) * 6 - 1 name 6 different column blocks in increasing order, all within 4 * g * 6 to 4 * (g + 1) * 6 - 1. `second_blocks`: in block row j, slots g * 3 to (g + 1) * 3 - 1 name 3 different column blocks in increasing order, all within 4 * g * 3 to 4 * (g + 1) * 3 - 1.
All inputs are finite; a program needn't handle non-finite values.
Results may differ from the reference program's by a relative error of at most 0.0049.
Values may be sent and summed in bfloat16 or wider, within the bound.
A program may use at most 192 MiB of HBM per device.

```python
import jax
import jax.numpy as jnp
from jax import lax

D = 12288
F = 49152
BLK = 128
TOKENS = 768
S1 = 6
S2 = 3
N_ROW = 16
N_COL = 8


def pick_blocks(key, block_rows, groups, chosen):
    group_span = 4 * chosen
    key_list = jax.random.split(key, block_rows * groups)

    def one_list(single):
        return jnp.sort(jax.random.permutation(single, group_span)[:chosen])
    chosen_lists = jax.vmap(one_list)(key_list).reshape(block_rows, groups, chosen)
    offsets = (jnp.arange(groups, dtype=jnp.int32) * group_span)[None, :, None]
    return (chosen_lists.astype(jnp.int32) + offsets).reshape(block_rows, groups * chosen).astype(jnp.int32)


def draw_first_blocks(key, part):
    key = jax.random.fold_in(key, 11)
    return pick_blocks(key, D // BLK, F // BLK // (4 * S1), S1)


def draw_second_blocks(key, part):
    key = jax.random.fold_in(key, 23)
    return pick_blocks(key, F // BLK, D // BLK // (4 * S2), S2)


def level_of(own_key, shape, cuts, smallest, top_value):
    factor_of = 1.0
    for dim, shards_of in cuts:
        heights = jax.random.uniform(jax.random.fold_in(jax.random.fold_in(own_key, 6), dim), (shards_of,), jnp.float32, smallest / len(cuts), top_value / len(cuts))
        factor_of = factor_of * jnp.repeat(jnp.exp(heights), shape[dim] // shards_of).reshape((-1,) + (1,) * (len(shape) - 1 - dim))
    return factor_of


def bell_draw(key, dims, scale, reach, shards=(), kind=jnp.bfloat16):
    entries = jax.random.normal(key, dims, jnp.float32) * scale
    if len(shards) > 0:
        entries = level_of(key, dims, shards, -0.22, 0.18) * entries
    return jnp.clip(entries, min=-reach, max=reach).astype(kind)


def setup_inputs(seed: int = 0) -> dict:
    splits = jax.random.split(jax.random.key(seed), 7)
    return {
        "inputs": bell_draw(splits[0], (TOKENS, D), 1.0, 6.0, ((0, 16), (1, 8))),
        "first_values": bell_draw(splits[1], (D // BLK, N_ROW * S1, BLK, BLK), (D // 4) ** -0.5, 0.109375, ((0, 8), (1, 16))),
        "first_blocks": draw_first_blocks(jax.random.fold_in(splits[6], 71), 0),
        "second_values": bell_draw(splits[3], (F // BLK, N_COL * S2, BLK, BLK), (F // 4) ** -0.5, 0.0546875, ((0, 16), (1, 8))),
        "second_blocks": draw_second_blocks(jax.random.fold_in(splits[6], 71), 0),
        "cotangent": bell_draw(splits[5], (TOKENS, D), 1.0, 6.0, ((0, 16), (1, 8))),
    }


gelu_scale = 0.7978845608028654
gelu_cubic = 0.044715


def gelu_pair(pre_act):
    inner_arg = gelu_scale * (pre_act + gelu_cubic * pre_act * pre_act * pre_act)
    tanh_value = jnp.tanh(inner_arg)
    activated = 0.5 * pre_act * (1.0 + tanh_value)
    derivative = 0.5 * (1.0 + tanh_value) + 0.5 * pre_act * (1.0 - tanh_value * tanh_value) * gelu_scale * (1.0 + 3.0 * gelu_cubic * pre_act * pre_act)
    return activated, derivative


def spread(panels, values, blocks, out_blocks):
    row_count = panels.shape[0]
    side = values.shape[2]
    shaped = panels.reshape(row_count, values.shape[0], side)

    def add_row(row_index, running):
        source = shaped[:, row_index, :].astype(jnp.float32)
        weights = values[row_index].astype(jnp.float32)
        terms = jnp.einsum("tk,sko->tso", source, weights, precision=lax.Precision.HIGHEST)
        return running.at[:, blocks[row_index], :].add(terms)

    initial = jnp.zeros((row_count, out_blocks, side), jnp.float32)
    running = lax.fori_loop(0, values.shape[0], add_row, initial)
    return running.reshape(row_count, out_blocks * side)


def gather_back(out_grad, kept, values, blocks):
    row_count = out_grad.shape[0]
    side = values.shape[2]
    grad_shaped = out_grad.reshape(row_count, -1, side)
    kept_shaped = kept.reshape(row_count, values.shape[0], side)

    def one_row(row_index):
        picked = grad_shaped[:, blocks[row_index], :].astype(jnp.float32)
        weights = values[row_index].astype(jnp.float32)
        backward = jnp.einsum("tso,sko->tk", picked, weights, precision=lax.Precision.HIGHEST)
        source = kept_shaped[:, row_index, :].astype(jnp.float32)
        grad_blocks = jnp.einsum("tk,tso->sko", source, picked, precision=lax.Precision.HIGHEST)
        return backward, grad_blocks

    backward, grad_blocks = lax.map(one_row, jnp.arange(values.shape[0], dtype=jnp.int32))
    backward = jnp.transpose(backward, (1, 0, 2)).reshape(row_count, values.shape[0] * side)
    return backward, grad_blocks


def reference(inputs, first_values, first_blocks, second_values, second_blocks, cotangent):
    pre_act = spread(inputs, first_values, first_blocks.astype(jnp.int32), F // BLK)
    activated, derivative = gelu_pair(pre_act)
    hidden = activated.astype(jnp.bfloat16)
    outputs = spread(hidden, second_values, second_blocks.astype(jnp.int32), D // BLK).astype(jnp.bfloat16)
    hidden_grad, second_grad = gather_back(cotangent, hidden, second_values, second_blocks.astype(jnp.int32))
    pre_grad = (hidden_grad * derivative).astype(jnp.bfloat16)
    input_grad, first_grad = gather_back(pre_grad, inputs, first_values, first_blocks.astype(jnp.int32))
    return outputs, input_grad.astype(jnp.bfloat16), first_grad.astype(jnp.bfloat16), second_grad.astype(jnp.bfloat16)
```

```python
import jax
import jax.numpy as jnp
from jax import lax
from jax.experimental import pallas as pl
from jax.experimental.pallas import tpu as pltpu
from jax.sharding import PartitionSpec as P

MESH = pl.DeviceIdType.MESH
gelu_scale = 0.7978845608028654
gelu_cubic = 0.044715

BLK = 128
CW = 256
NQ = 12
NU = 2 * NQ
NS = 8
NP = 4
SH = 96
RY = 64
OWN = 48
DW = 1536
S2, S3, S4, A2, A3, A4 = 2, 3, 4, 5, 6, 7
TICKS = NU + A4


def gelu_pair(pre_act):
    inner_arg = gelu_scale * (pre_act + gelu_cubic * pre_act * pre_act * pre_act)
    tanh_value = jnp.tanh(inner_arg)
    activated = 0.5 * pre_act * (1.0 + tanh_value)
    derivative = 0.5 * (1.0 + tanh_value) + 0.5 * pre_act * (
        1.0 - tanh_value * tanh_value
    ) * gelu_scale * (1.0 + 3.0 * gelu_cubic * pre_act * pre_act)
    return (activated, derivative)


def f32(v):
    return v.astype(jnp.float32)


def bf16(v):
    return v.astype(jnp.bfloat16)


def dot(a, b, ca, cb):
    return lax.dot_general(a, b, (((ca,), (cb,)), ((), ())), preferred_element_type=jnp.float32)


def kernel(
    inv1, inv2, pick1, pick2, x_in, c_in, v1_hbm, v2_hbm,
    out_ref, ig_ref, fg_ref, sg_ref,
    panel, cblk, xt, v1, v2, wd1, wd2, part, sy_y, szo_y, sz_y, szo_z, sz_z, sy_z,
    ry_y, rzo_y, rz_y, rzo_z, rz_z, ry_z,
    gath, deriv, acc, fgd, rd, rq, ro, rx, ryl, tf,
    v_sem, rs_s, rs_r, ag_s, ag_r, rg_s, rg_r, rr_s, rr_r,
):
    row, col = lax.axis_index("row"), lax.axis_index("col")
    x, yl, core = row // 4, (row // 2) % 2, row % 2
    z, y = col // 2, col % 2
    zp, zm, zo = (z + 1) % 4, (z + 3) % 4, (z + 2) % 4
    xp, xm, xo = (x + 1) % 4, (x + 3) % 4, (x + 2) % 4
    yo, ylo, co = 1 - y, 1 - yl, 1 - core

    def at_row(ax, ayl, ac):
        return (ax * 2 + ayl) * 2 + ac

    dev_z = ((row, zp * 2 + y), (row, zm * 2 + y))
    dev_y = (row, z * 2 + yo)
    dev_x = ((at_row(xp, yl, core), col), (at_row(xm, yl, core), col))
    dev_yl = (at_row(x, ylo, core), col)
    dev_c = (at_row(x, yl, co), col)

    barrier = pltpu.get_barrier_semaphore()
    for dev in (*dev_z, dev_y, *dev_x, dev_yl, dev_c):
        pl.semaphore_signal(barrier, inc=1, device_id=dev, device_id_type=MESH)

    def copy(src, dst, send, recv, dev):
        return pltpu.make_async_remote_copy(
            src_ref=src, dst_ref=dst, send_sem=send, recv_sem=recv, device_id=dev, device_id_type=MESH
        )

    load1 = pltpu.make_async_copy(v1_hbm, v1.at[pl.ds(0, 72)], v_sem.at[0])
    load2 = pltpu.make_async_copy(v2_hbm, v2.at[pl.ds(0, 72)], v_sem.at[1])
    load1.start()
    load2.start()
    v1[72] = jnp.zeros((BLK, BLK), jnp.bfloat16)
    v2[72] = jnp.zeros((BLK, BLK), jnp.bfloat16)
    panel[0, row] = x_in[...]
    panel[1, row] = c_in[...]
    acc[...] = jnp.zeros(acc.shape, jnp.float32)
    pl.semaphore_wait(barrier, 7)

    halves = (pl.ds(0, DW // 2), pl.ds(DW // 2, DW // 2))

    def rg(p, k, src, dev):
        return copy(src, src, rg_s.at[p, k], rg_r.at[p, k], dev)

    def rg_piece(p, ax, ayl, ac=None):
        return panel.at[p, at_row(ax, ayl, core if ac is None else ac)]

    near, far = (xm, xp), (xp, xm)

    order = [(x, yl), (x, ylo), (xm, yl), (xp, yl), (xm, ylo), (xp, ylo), (xo, yl), (xo, ylo)]

    def to_core(p, i):
        return rg(p, 9 + i, rg_piece(p, *order[i]), dev_c)

    def gather_step(p, step):
        if step == 0:
            own = rg_piece(p, x, yl)
            rg(p, 0, own, dev_yl).start()
            for d in range(2):
                rg(p, 1 + d, own, dev_x[d]).start()
            to_core(p, 0).start()
        if step == 1:
            rg(p, 0, rg_piece(p, x, ylo), dev_yl).wait_recv()
            other = rg_piece(p, x, ylo)
            for d in range(2):
                rg(p, 3 + d, other, dev_x[d]).start()
            to_core(p, 1).start()
        if step in (2, 3):
            side = (yl, ylo)[step - 2]
            for d in range(2):
                piece = rg_piece(p, near[d], side)
                rg(p, 1 + 2 * (step - 2) + d, piece, dev_x[d]).wait_recv()
                half = piece.at[:, halves[d]]
                rg(p, 5 + 2 * (step - 2) + d, half, dev_x[d]).start()
                to_core(p, 2 + 2 * (step - 2) + d).start()
        if step == 4:
            for s, side in enumerate((yl, ylo)):
                for d in range(2):
                    half = rg_piece(p, xo, side).at[:, halves[d]]
                    rg(p, 5 + 2 * s + d, half, dev_x[d]).wait_recv()
                to_core(p, 6 + s).start()
        if step == 5:
            own = rg_piece(p, x, yl)
            rg(p, 0, own, dev_yl).wait_send()
            for s, side in enumerate((yl, ylo)):
                for d in range(2):
                    rg(p, 1 + 2 * s + d, rg_piece(p, x, side), dev_x[d]).wait_send()
                    half = rg_piece(p, near[d], side).at[:, halves[d]]
                    rg(p, 5 + 2 * s + d, half, dev_x[d]).wait_send()
            for i in range(8):
                to_core(p, i).wait_send()
                rg(p, 9 + i, rg_piece(p, *order[i], co), dev_c).wait_recv()

    for step in range(6):
        gather_step(0, step)
    load1.wait()
    load2.wait()
    xt[...] = panel[0].reshape(16 * OWN, DW).T

    def dense1(q):
        for i in range(12):
            for h in range(2):
                wd1[pl.ds(i * BLK, BLK), pl.ds(h * BLK, BLK)] = v1[inv1[i, q * 2 + h]]
        return wd1[...]

    def dense2(q):
        for h in range(2):
            for i in range(12):
                wd2[pl.ds(h * BLK, BLK), pl.ds(i * BLK, BLK)] = v2[inv2[q * 2 + h, i]]
        return wd2[...]

    ya, za = pl.ds(0, RY), pl.ds(RY, SH - RY)
    hc = (pl.ds(0, CW // 2), pl.ds(CW // 2, CW // 2))
    tgt = (zp, zm)

    def rs(s, k, src, dst, dev):
        return copy(src, dst, rs_s.at[s, k], rs_r.at[s, k], dev)

    def rs_y_y(u):
        return rs(u % NS, 0, sy_y.at[u % 2], ry_y.at[u % NS], dev_y)

    def rs_zo_y(u, d):
        return rs(u % NS, 1 + d, szo_y.at[u % 2, d], rzo_y.at[u % NS, d], dev_z[d])

    def rs_z_y(u, d):
        return rs(u % NS, 3 + d, sz_y.at[u % 2, d], rz_y.at[u % NS, d], dev_z[d])

    def rs_zo_z(u, d):
        return rs(u % NS, 5 + d, szo_z.at[u % 2, d], rzo_z.at[u % NS, d], dev_z[d])

    def rs_z_z(u, d):
        return rs(u % NS, 7 + d, sz_z.at[u % 2, d], rz_z.at[u % NS, d], dev_z[d])

    def rs_y_z(u):
        return rs(u % NS, 9, sy_z.at[u % 2], ry_z.at[u % NS], dev_y)

    def ag(s, k, ref, dev):
        return copy(ref, ref, ag_s.at[s, k], ag_r.at[s, k], dev)

    src_z = (zm, zp)

    def ag_y_y(s, side):
        return ag(s, 0, gath.at[s, z, side, ya], dev_y)

    def ag_z_y(s, d, at):
        return ag(s, 1 + d, gath.at[s, at, :, ya], dev_z[d])

    def ag_zo_y(s, d, at):
        return ag(s, 3 + d, gath.at[s, at, :, ya, hc[d]], dev_z[d])

    def ag_z_z(s, d, at):
        return ag(s, 5 + d, gath.at[s, at, y, za], dev_z[d])

    def ag_zo_z(s, d, at):
        return ag(s, 7 + d, gath.at[s, at, y, za, hc[d]], dev_z[d])

    def ag_y_z(s, side):
        return ag(s, 9, gath.at[s, :, side, za], dev_y)

    def product(u):
        sp, s2 = u % NP, u % 2

        @pl.when(u < NQ)
        def _():
            r = dot(panel[0].reshape(16 * OWN, DW), dense1(u), 1, 0)
            part[sp] = r.reshape(4, 2, SH, CW)

        @pl.when(u >= NQ)
        def _():
            r = dot(panel[1].reshape(16 * OWN, DW), dense2(u - NQ), 1, 1)
            part[sp] = r.reshape(4, 2, SH, CW)

        sy_y[s2] = bf16(part[sp, :, yo, ya])
        rs_y_y(u).start()
        for d in range(2):
            szo_z[s2, d] = bf16(part[sp, zo, :, za, hc[d]])
            rs_zo_z(u, d).start()

    def stage2(u):
        s, sp, s2 = u % NS, u % NP, u % 2
        rs_y_y(u).wait()
        for d in range(2):
            szo_y[s2, d] = bf16(part[sp, zo, y, ya, hc[d]] + f32(ry_y[s, zo, :, hc[d]]))
            rs_zo_y(u, d).start()
        for d in range(2):
            rs_zo_z(u, d).wait()
            sz_z[s2, d, :, :, hc[d]] = bf16(part[sp, tgt[d], :, za, hc[d]] + f32(rzo_z[s, d]))
            sz_z[s2, d, :, :, hc[1 - d]] = bf16(part[sp, tgt[d], :, za, hc[1 - d]])
            rs_z_z(u, d).start()

    def stage3(u):
        s, sp, s2 = u % NS, u % NP, u % 2
        for d in range(2):
            rs_zo_y(u, d).wait()
            for e in range(2):
                total = part[sp, tgt[d], y, ya, hc[e]] + f32(ry_y[s, tgt[d], :, hc[e]])
                if e == d:
                    total = total + f32(rzo_y[s, d])
                sz_y[s2, d, :, hc[e]] = bf16(total)
            rs_z_y(u, d).start()
        for d in range(2):
            rs_z_z(u, d).wait()
        sy_z[s2] = bf16(part[sp, z, yo, za] + f32(rz_z[s, 0, yo]) + f32(rz_z[s, 1, yo]))
        rs_y_z(u).start()

    def stage4(u):
        s, sp = u % NS, u % NP
        for d in range(2):
            rs_z_y(u, d).wait()
        sum_y = part[sp, z, y, ya] + f32(ry_y[s, z]) + f32(rz_y[s, 0]) + f32(rz_y[s, 1])
        rs_y_z(u).wait()
        sum_z = part[sp, z, y, za] + f32(rz_z[s, 0, y]) + f32(rz_z[s, 1, y]) + f32(ry_z[s])

        @pl.when(u < NQ)
        def _():
            for rows, total in ((ya, sum_y), (za, sum_z)):
                activated, derivative = gelu_pair(total)
                gath[s, z, y, rows] = bf16(activated)
                deriv[u, rows] = derivative

        @pl.when(u >= NQ)
        def _():
            for rows, total in ((ya, sum_y), (za, sum_z)):
                gath[s, z, y, rows] = bf16(total * deriv[u - NQ, rows])

        ag_y_y(s, y).start()
        for d in range(2):
            ag_z_z(s, d, z).start()

    def gather2(u):
        s = u % NS
        ag_y_y(s, yo).wait_recv()
        for d in range(2):
            ag_z_y(s, d, z).start()
        for d in range(2):
            ag_z_z(s, d, src_z[d]).wait_recv()
            ag_zo_z(s, d, src_z[d]).start()

    def gather3(u):
        s = u % NS
        for d in range(2):
            ag_z_y(s, d, src_z[d]).wait_recv()
            ag_zo_y(s, d, src_z[d]).start()
        for d in range(2):
            ag_zo_z(s, d, zo).wait_recv()
        ag_y_z(s, y).start()

    def gather4(u):
        s = u % NS
        for d in range(2):
            ag_zo_y(s, d, zo).wait_recv()
        ag_y_z(s, yo).wait_recv()
        ag_y_y(s, y).wait_send()
        ag_y_z(s, y).wait_send()
        for d in range(2):
            ag_z_y(s, d, z).wait_send()
            ag_zo_y(s, d, src_z[d]).wait_send()
            ag_z_z(s, d, z).wait_send()
            ag_zo_z(s, d, src_z[d]).wait_send()

    def use(u):
        s = u % NS

        @pl.when(u < NQ)
        def _():
            hidden = gath[s].reshape(8 * SH, CW)
            r = dot(hidden, dense2(u), 1, 0)
            acc[0] += r.reshape(8, 2, OWN, DW)
            flipped = hidden.T
            for h in range(2):
                j = u * 2 + h
                picked = jnp.concatenate(
                    [
                        cblk[pick2[j, k]]
                        for k in range(3)
                    ],
                    axis=1,
                )
                g = bf16(dot(flipped[h * BLK : (h + 1) * BLK], picked, 1, 0))
                for k in range(3):
                    sg_ref[j, k] = g[:, k * BLK : (k + 1) * BLK]

        @pl.when(u >= NQ)
        def _():
            q = u - NQ
            grad = gath[s].reshape(8 * SH, CW)
            r = dot(grad, dense1(q), 1, 1)
            acc[1] += r.reshape(8, 2, OWN, DW)
            g = bf16(dot(xt[...], grad, 1, 0))
            for h in range(2):
                fgd[q * 2 + h] = g[:, h * BLK : (h + 1) * BLK]

    hd = (pl.ds(0, DW // 2), pl.ds(DW // 2, DW // 2))
    tgt_x = (xp, xm)

    def rr(p, k, src, dst, dev):
        return copy(src, dst, rr_s.at[p, k], rr_r.at[p, k], dev)

    def rr_core(p):
        return rr(p, 0, acc.at[p, :, co], rd.at[p], dev_c)

    def rr_xo(p, d):
        return rr(p, 1 + d, rq.at[xo, :, :, hd[d]], ro.at[p, d], dev_x[d])

    def rr_x(p, d):
        return rr(p, 3 + d, rq.at[tgt_x[d]], rx.at[p, d], dev_x[d])

    def rr_yl(p):
        return rr(p, 5, tf, ryl.at[p], dev_yl)

    def own_sum(p, ax, ayl):
        return acc[p, ax * 2 + ayl, core] + rd[p, ax * 2 + ayl]

    def scatter_step(p, step):
        if step == 0:
            rr_core(p).start()
        if step == 1:
            rr_core(p).wait()
            for at in (xo, xp, xm):
                for b in range(2):
                    rq[at, b] = bf16(own_sum(p, at, b))
                if at is xo:
                    for d in range(2):
                        rr_xo(p, d).start()
        if step == 2:
            for d in range(2):
                rr_xo(p, d).wait()
                for b in range(2):
                    own = acc[p, tgt_x[d] * 2 + b, core, :, hd[d]] + rd[p, tgt_x[d] * 2 + b, :, hd[d]]
                    rq[tgt_x[d], b, :, hd[d]] = bf16(own + f32(ro[p, d, b]))
                rr_x(p, d).start()
        if step == 3:
            for d in range(2):
                rr_x(p, d).wait()
            tf[...] = bf16(own_sum(p, x, ylo) + f32(rx[p, 0, ylo]) + f32(rx[p, 1, ylo]))
            rr_yl(p).start()
        if step == 4:
            rr_yl(p).wait()
            total = own_sum(p, x, yl) + f32(rx[p, 0, yl]) + f32(rx[p, 1, yl]) + f32(ryl[p])
            (out_ref, ig_ref)[p][...] = bf16(total)

    def tick(t, carry):
        def run(offset, fn):
            u = t - offset

            @pl.when(jnp.logical_and(u >= 0, u < NU))
            def _():
                fn(u)

        run(A4, gather4)
        run(A3, gather3)
        run(A2, gather2)
        run(S4, stage4)
        run(S3, stage3)
        run(S2, stage2)
        for step in range(6):
            @pl.when(t == 1 + step)
            def _():
                gather_step(1, step)
        @pl.when(t == 7)
        def _():
            for c in range(12):
                cblk[c] = panel[1, :, :, c * BLK : (c + 1) * BLK].reshape(16 * OWN, BLK)

        for step in range(5):
            @pl.when(t == NQ + A4 + step)
            def _():
                scatter_step(0, step)
        run(0, product)
        run(A4, use)
        return carry

    lax.fori_loop(0, TICKS, tick, 0)
    scatter_step(1, 0)
    for i in range(12):
        for k in range(6):
            fg_ref[i, k] = fgd[pick1[i, k], pl.ds(i * BLK, BLK), :]
    for step in range(1, 5):
        scatter_step(1, step)


def shards(inputs, first_values, first_blocks, second_values, second_blocks, cotangent):
    pick1 = first_blocks - lax.axis_index("row") * 24
    pick2 = second_blocks - lax.axis_index("col") * 12

    def slot_table(pick, width):
        rows, slots = pick.shape
        number = jnp.arange(rows * slots, dtype=jnp.int32).reshape(rows, slots) - rows * slots
        hit = pick[:, :, None] == jnp.arange(width, dtype=jnp.int32)
        return rows * slots + jnp.sum(jnp.where(hit, number[:, :, None], 0), axis=1)

    inv1 = slot_table(pick1, 24)
    inv2 = slot_table(pick2, 12)
    bf, fl = jnp.bfloat16, jnp.float32
    smem = pl.BlockSpec(memory_space=pltpu.SMEM)
    vmem = pl.BlockSpec(memory_space=pltpu.VMEM)
    dma = pltpu.SemaphoreType.DMA
    v1 = first_values.reshape(72, BLK, BLK)
    v2 = second_values.reshape(72, BLK, BLK)
    return pl.pallas_call(
        kernel,
        out_shape=(
            jax.ShapeDtypeStruct((OWN, DW), bf),
            jax.ShapeDtypeStruct((OWN, DW), bf),
            jax.ShapeDtypeStruct((12, 6, BLK, BLK), bf),
            jax.ShapeDtypeStruct((24, 3, BLK, BLK), bf),
        ),
        in_specs=[smem] * 4 + [vmem] * 2 + [pl.BlockSpec(memory_space=pl.ANY)] * 2,
        out_specs=(vmem,) * 4,
        scratch_shapes=[
            pltpu.VMEM((2, 16, OWN, DW), bf),
            pltpu.VMEM((12, 16 * OWN, BLK), bf),
            pltpu.VMEM((DW, 16 * OWN), bf),
            pltpu.VMEM((73, BLK, BLK), bf),
            pltpu.VMEM((73, BLK, BLK), bf),
            pltpu.VMEM((DW, CW), bf),
            pltpu.VMEM((CW, DW), bf),
            pltpu.VMEM((NP, 4, 2, SH, CW), fl),
            pltpu.VMEM((2, 4, RY, CW), bf),
            pltpu.VMEM((2, 2, RY, CW // 2), bf),
            pltpu.VMEM((2, 2, RY, CW), bf),
            pltpu.VMEM((2, 2, 2, SH - RY, CW // 2), bf),
            pltpu.VMEM((2, 2, 2, SH - RY, CW), bf),
            pltpu.VMEM((2, SH - RY, CW), bf),
            pltpu.VMEM((NS, 4, RY, CW), bf),
            pltpu.VMEM((NS, 2, RY, CW // 2), bf),
            pltpu.VMEM((NS, 2, RY, CW), bf),
            pltpu.VMEM((NS, 2, 2, SH - RY, CW // 2), bf),
            pltpu.VMEM((NS, 2, 2, SH - RY, CW), bf),
            pltpu.VMEM((NS, SH - RY, CW), bf),
            pltpu.VMEM((NS, 4, 2, SH, CW), bf),
            pltpu.VMEM((NQ, SH, CW), fl),
            pltpu.VMEM((2, 8, 2, OWN, DW), fl),
            pltpu.VMEM((24, DW, BLK), bf),
            pltpu.VMEM((2, 8, OWN, DW), fl),
            pltpu.VMEM((4, 2, OWN, DW), bf),
            pltpu.VMEM((2, 2, 2, OWN, DW // 2), bf),
            pltpu.VMEM((2, 2, 2, OWN, DW), bf),
            pltpu.VMEM((2, OWN, DW), bf),
            pltpu.VMEM((OWN, DW), bf),
            dma((2,)),
            dma((NS, 10)), dma((NS, 10)), dma((NS, 10)), dma((NS, 10)),
            dma((2, 17)), dma((2, 17)), dma((2, 6)), dma((2, 6)),
        ],
        compiler_params=pltpu.CompilerParams(
            collective_id=1, has_side_effects=True, vmem_limit_bytes=62 * 2**20
        ),
        name="sparse_ffn",
    )(inv1, inv2, pick1, pick2, inputs, cotangent, v1, v2)


def solution(mesh):
    placed = (
        P("row", "col"),
        P("col", "row", None, None),
        P("col", "row"),
        P("row", "col", None, None),
        P("row", "col"),
        P("row", "col"),
    )
    return jax.shard_map(
        shards,
        mesh=mesh,
        in_specs=placed,
        out_specs=(
            P("row", "col"),
            P("row", "col"),
            P("col", "row", None, None),
            P("row", "col", None, None),
        ),
        check_vma=False,
    )
```

```python
import jax
import jax.numpy as jnp
from jax import lax
from jax.experimental import pallas as pl
from jax.experimental.pallas import tpu as pltpu
from jax.sharding import PartitionSpec as P

MESH = pl.DeviceIdType.MESH
gelu_scale = 0.7978845608028654
gelu_cubic = 0.044715

BLK = 128
NG = 3
NC = 4
CB = 6
CW = CB * BLK
NN = NG * NC
NU = 2 * NN
NS = 12
NA = 13
NT = 3
NP = 9
GR = 16
SR = 2 * GR
OWN = NG * GR
DW = 1536
S2, S3, S4 = 3, 6, 9
A2, A3, A4 = 3, 6, 9
AG1, AG2 = NN + 1, 3 * NN
TICKS = AG2 + NN + A4
SG = AG1 + 2 * NN + A4 - 1


def gelu_pair(pre_act):
    inner_arg = gelu_scale * (pre_act + gelu_cubic * pre_act * pre_act * pre_act)
    tanh_value = jnp.tanh(inner_arg)
    activated = 0.5 * pre_act * (1.0 + tanh_value)
    derivative = 0.5 * (1.0 + tanh_value) + 0.5 * pre_act * (
        1.0 - tanh_value * tanh_value
    ) * gelu_scale * (1.0 + 3.0 * gelu_cubic * pre_act * pre_act)
    return (activated, derivative)


def f32(v):
    return v.astype(jnp.float32)


def bf16(v):
    return v.astype(jnp.bfloat16)


def dot(a, b, ca, cb):
    return lax.dot_general(a, b, (((ca,), (cb,)), ((), ())), preferred_element_type=jnp.float32)


def kernel(
    inv1, inv2, pick1, pick2, x_in, c_in, v1_hbm, v2_hbm,
    out_ref, ig_ref, fg_ref, sg_ref,
    panel, cblk, xt, v1, v2, wd1, wd2, part, sy_y, szo_y, sz_y, szo_z, sz_z, sy_z,
    ry_y, rzo_y, rz_y, rzo_z, rz_z, ry_z,
    gath, deriv, acc, rd, rq, rx, ryl, tf, sgb, fgb,
    v_sem, rs_s, rs_r, ag_s, ag_r, rg_s, rg_r, rr_s, rr_r,
):
    row, col = lax.axis_index("row"), lax.axis_index("col")
    x, yl, core = row // 4, (row // 2) % 2, row % 2
    z, y = col // 2, col % 2
    zp, zm, zo = (z + 1) % 4, (z + 3) % 4, (z + 2) % 4
    xp, xm, xo = (x + 1) % 4, (x + 3) % 4, (x + 2) % 4
    yo, ylo, co = 1 - y, 1 - yl, 1 - core

    def at_row(ax, ayl, ac):
        return (ax * 2 + ayl) * 2 + ac

    dev_z = ((row, zp * 2 + y), (row, zm * 2 + y))
    dev_y = (row, z * 2 + yo)
    dev_row = [(at_row(ax, yl, core), col) for ax in (xp, xm, xo)]
    dev_row += [(at_row(ax, ylo, core), col) for ax in (x, xp, xm, xo)]
    dev_row += [(at_row(x, yl, co), col)]

    barrier = pltpu.get_barrier_semaphore()
    for dev in (*dev_z, dev_y, *dev_row):
        pl.semaphore_signal(barrier, inc=1, device_id=dev, device_id_type=MESH)

    def copy(src, dst, send, recv, dev):
        return pltpu.make_async_remote_copy(
            src_ref=src, dst_ref=dst, send_sem=send, recv_sem=recv, device_id=dev, device_id_type=MESH
        )

    load1 = pltpu.make_async_copy(v1_hbm, v1.at[pl.ds(0, 72)], v_sem.at[0])
    load2 = pltpu.make_async_copy(v2_hbm, v2.at[pl.ds(0, 72)], v_sem.at[1])
    load1.start()
    load2.start()
    for g in range(NG):
        panel[0, g, row] = x_in[pl.ds(g * GR, GR)]
        panel[1, g, row] = c_in[pl.ds(g * GR, GR)]
    pl.semaphore_wait(barrier, 11)


    order = [(x, yl), (x, ylo), (xp, yl), (xm, yl), (xo, yl), (xp, ylo), (xm, ylo), (xo, ylo)]
    all_x = (xp, xm, xo)
    from_x = (xm, xp, xo)

    def gather_step(p, g, step, direct=False):
        def rg(k, src, ax, ayl, ac=core):
            return copy(src, src, rg_s.at[p, g, k], rg_r.at[p, g, k], (at_row(ax, ayl, ac), col))

        def piece(ax, ayl, ac=core):
            return panel.at[p, g, at_row(ax, ayl, ac)]

        def over_yl(side):
            return rg(0, piece(x, side), x, ylo)

        def own_x(d, at):
            return rg(1 + d, piece(at, yl), all_x[d], yl)

        def other_x(d, at):
            if direct:
                return rg(4 + d, piece(at, ylo if at is not x else yl), all_x[d], ylo)
            return rg(4 + d, piece(at, ylo), all_x[d], yl)

        def to_core(i, ac=core):
            return rg(7 + i, piece(*order[i], ac), x, yl, co)

        if step == 0:
            over_yl(yl).start()
            for d in range(3):
                own_x(d, x).start()
            if direct:
                for d in range(3):
                    other_x(d, x).start()
            to_core(0).start()
        if step == 1:
            over_yl(ylo).wait_recv()
            if not direct:
                for d in range(3):
                    other_x(d, x).start()
            to_core(1).start()
        if step == 2:
            for d in range(3):
                own_x(d, from_x[d]).wait_recv()
                to_core(2 + (1, 0, 2)[d]).start()
        if step == 3:
            for d in range(3):
                other_x(d, from_x[d]).wait_recv()
                to_core(5 + (1, 0, 2)[d]).start()
        if step == 4:
            over_yl(yl).wait_send()
            for d in range(3):
                own_x(d, x).wait_send()
                other_x(d, x).wait_send()
            for i in range(8):
                to_core(i).wait_send()
                to_core(i, co).wait_recv()

    for step in range(5):
        gather_step(0, 0, step, direct=True)
        if step == 0:
            v1[72] = jnp.zeros((BLK, BLK), jnp.bfloat16)
            v2[72] = jnp.zeros((BLK, BLK), jnp.bfloat16)
            acc[...] = jnp.zeros(acc.shape, jnp.float32)
        if step == 1:
            gather_step(0, 1, 0)
        if step == 3:
            gather_step(0, 1, 1)
            gather_step(0, 2, 0)
    load1.wait()
    load2.wait()

    def dense1(c):
        for i in range(12):
            for h in range(CB):
                wd1[pl.ds(i * BLK, BLK), pl.ds(h * BLK, BLK)] = v1[inv1[i, c * CB + h]]
        return wd1[...]

    def dense2(c):
        for h in range(CB):
            for i in range(12):
                wd2[pl.ds(h * BLK, BLK), pl.ds(i * BLK, BLK)] = v2[inv2[c * CB + h, i]]
        return wd2[...]

    ya, za = pl.ds(0, GR), pl.ds(GR, GR)
    hc = (pl.ds(0, CW // 2), pl.ds(CW // 2, CW // 2))
    tgt, src_z = (zp, zm), (zm, zp)

    def rs(u, k, src, dst, dev):
        return copy(src, dst, rs_s.at[u % NS, k], rs_r.at[u % NS, k], dev)

    def rs_y_y(u):
        return rs(u, 0, sy_y.at[u % NT], ry_y.at[u % NS], dev_y)

    def rs_zo_y(u, d):
        return rs(u, 1 + d, szo_y.at[u % NT, d], rzo_y.at[u % NS, d], dev_z[d])

    def rs_z_y(u, d):
        return rs(u, 3 + d, sz_y.at[u % NT, d], rz_y.at[u % NS, d], dev_z[d])

    def rs_zo_z(u, d):
        return rs(u, 5 + d, szo_z.at[u % NT, d], rzo_z.at[u % NS, d], dev_z[d])

    def rs_z_z(u, d):
        return rs(u, 7 + d, sz_z.at[u % NT, d], rz_z.at[u % NS, d], dev_z[d])

    def rs_y_z(u):
        return rs(u, 9, sy_z.at[u % NT], ry_z.at[u % NS], dev_y)

    def product(u):
        sp, s2 = u % NP, u % NT
        g, c = (u // NC) % NG, u % NC

        @pl.when(u < NN)
        def _():
            r = dot(panel[0, g].reshape(16 * GR, DW), dense1(c), 1, 0)
            part[sp] = r.reshape(4, 2, SR, CW)

        @pl.when(u >= NN)
        def _():
            r = dot(panel[1, g].reshape(16 * GR, DW), dense2(c), 1, 1)
            part[sp] = r.reshape(4, 2, SR, CW)

        sy_y[s2] = bf16(part[sp, :, yo, ya])
        rs_y_y(u).start()
        for d in range(2):
            szo_z[s2, d] = bf16(part[sp, zo, :, za, hc[d]])
            rs_zo_z(u, d).start()

    def stage2(u):
        s, sp, s2 = u % NS, u % NP, u % NT
        rs_y_y(u).wait()
        for d in range(2):
            szo_y[s2, d] = bf16(part[sp, zo, y, ya, hc[d]] + f32(ry_y[s, zo, :, hc[d]]))
            rs_zo_y(u, d).start()
        for d in range(2):
            rs_zo_z(u, d).wait()
            sz_z[s2, d, :, :, hc[d]] = bf16(part[sp, tgt[d], :, za, hc[d]] + f32(rzo_z[s, d]))
            sz_z[s2, d, :, :, hc[1 - d]] = bf16(part[sp, tgt[d], :, za, hc[1 - d]])
            rs_z_z(u, d).start()

    def stage3(u):
        s, sp, s2 = u % NS, u % NP, u % NT
        for d in range(2):
            rs_zo_y(u, d).wait()
            for e in range(2):
                total = part[sp, tgt[d], y, ya, hc[e]] + f32(ry_y[s, tgt[d], :, hc[e]])
                if e == d:
                    total = total + f32(rzo_y[s, d])
                sz_y[s2, d, :, hc[e]] = bf16(total)
            rs_z_y(u, d).start()
        for d in range(2):
            rs_z_z(u, d).wait()
        sy_z[s2] = bf16(part[sp, z, yo, za] + f32(rz_z[s, 0, yo]) + f32(rz_z[s, 1, yo]))
        rs_y_z(u).start()

    def stage4(u):
        s, sp = u % NS, u % NP
        g, c = (u // NC) % NG, u % NC
        for d in range(2):
            rs_z_y(u, d).wait()
        sum_y = part[sp, z, y, ya] + f32(ry_y[s, z]) + f32(rz_y[s, 0]) + f32(rz_y[s, 1])
        rs_y_z(u).wait()
        sum_z = part[sp, z, y, za] + f32(rz_z[s, 0, y]) + f32(rz_z[s, 1, y]) + f32(ry_z[s])

        def keep(p, rows, value):
            for b in range(CB):
                gath[p, c * CB + b, g, z, y, rows] = bf16(value[:, b * BLK : (b + 1) * BLK])

        @pl.when(u < NN)
        def _():
            for rows, total in ((ya, sum_y), (za, sum_z)):
                activated, derivative = gelu_pair(total)
                keep(0, rows, activated)
                deriv[u, rows] = derivative

        @pl.when(u >= NN)
        def _():
            for rows, total in ((ya, sum_y), (za, sum_z)):
                keep(1, rows, total * deriv[u - NN, rows])

    def ag_of(u):
        p, g, c = u // NN, (u // NC) % NG, u % NC
        yb = gath.at[p, pl.ds(c * CB, 4), g]
        zb = gath.at[p, pl.ds(c * CB + 4, 2), g]
        yh = (gath.at[p, pl.ds(c * CB, 2), g], gath.at[p, pl.ds(c * CB + 2, 2), g])
        zh = (gath.at[p, pl.ds(c * CB + 4, 1), g], gath.at[p, pl.ds(c * CB + 5, 1), g])

        def ag(k, ref, dev):
            return copy(ref, ref, ag_s.at[u % NA, k], ag_r.at[u % NA, k], dev)

        return (
            lambda side: ag(0, yb.at[:, z, side], dev_y),
            lambda d, at: ag(1 + d, yb.at[:, at], dev_z[d]),
            lambda d, at: ag(3 + d, yh[d].at[:, at], dev_z[d]),
            lambda d, at: ag(5 + d, zb.at[:, at, y], dev_z[d]),
            lambda d, at: ag(7 + d, zh[d].at[:, at, y], dev_z[d]),
            lambda side: ag(9, zb.at[:, :, side], dev_y),
        )

    def gather1(u):
        y_y, z_y, zo_y, z_z, zo_z, y_z = ag_of(u)
        y_y(y).start()
        for d in range(2):
            z_z(d, z).start()

    def gather2(u):
        y_y, z_y, zo_y, z_z, zo_z, y_z = ag_of(u)
        y_y(yo).wait_recv()
        for d in range(2):
            z_y(d, z).start()
        for d in range(2):
            z_z(d, src_z[d]).wait_recv()
            zo_z(d, src_z[d]).start()

    def gather3(u):
        y_y, z_y, zo_y, z_z, zo_z, y_z = ag_of(u)
        for d in range(2):
            z_y(d, src_z[d]).wait_recv()
            zo_y(d, src_z[d]).start()
        for d in range(2):
            zo_z(d, zo).wait_recv()
        y_z(y).start()

    def gather4(u):
        y_y, z_y, zo_y, z_z, zo_z, y_z = ag_of(u)
        for d in range(2):
            zo_y(d, zo).wait_recv()
        y_z(yo).wait_recv()
        y_y(y).wait_send()
        y_z(y).wait_send()
        for d in range(2):
            z_y(d, z).wait_send()
            zo_y(d, src_z[d]).wait_send()
            z_z(d, z).wait_send()
            zo_z(d, src_z[d]).wait_send()

    def use(u):
        p, g, c = u // NN, (u // NC) % NG, u % NC
        rows = jnp.concatenate([gath[p, c * CB + b, g].reshape(16 * GR, BLK) for b in range(CB)], axis=1)

        @pl.when(p == 0)
        def _():
            acc[0, g] += dot(rows, dense2(c), 1, 0).reshape(8, 2, GR, DW)

        @pl.when(p == 1)
        def _():
            acc[1, g] += dot(rows, dense1(c), 1, 1).reshape(8, 2, GR, DW)

    def second_out(j):
        return pltpu.make_async_copy(sgb.at[j % 2], sg_ref.at[j], v_sem.at[2 + j % 2])

    def second(j):
        flipped = gath[0, j].reshape(16 * OWN, BLK).T
        picked = jnp.concatenate([cblk[pick2[j, k]] for k in range(3)], axis=1)
        g = bf16(dot(flipped, picked, 1, 0))

        @pl.when(j >= 2)
        def _():
            second_out(j - 2).wait()

        for k in range(3):
            sgb[j % 2, k] = g[:, k * BLK : (k + 1) * BLK]
        second_out(j).start()

    def first_out(i):
        return pltpu.make_async_copy(fgb.at[i % 2], fg_ref.at[i], v_sem.at[4 + i % 2])

    def first(i):
        picked = jnp.concatenate([gath[1, pick1[i, k]].reshape(16 * OWN, BLK) for k in range(6)], axis=1)
        g = bf16(dot(xt[pl.ds(i * BLK, BLK), :], picked, 1, 0))
        if i >= 2:
            first_out(i - 2).wait()
        for k in range(6):
            fgb[i % 2, k] = g[:, k * BLK : (k + 1) * BLK]
        first_out(i).start()

    def scatter_step(p, g, step, direct=False):
        e = p * NG + g

        def rr(k, src, dst, ax, ayl, ac=core):
            return copy(src, dst, rr_s.at[e, k], rr_r.at[e, k], (at_row(ax, ayl, ac), col))

        def over_core():
            return rr(0, acc.at[p, g, :, co], rd.at[g], x, yl, co)

        def over_x(d, b=None):
            if b is None:
                return rr(1 + d, rq.at[g, all_x[d]], rx.at[g, d], all_x[d], yl)
            return rr(1 + 2 * d + b, rq.at[g, all_x[d], (yl, ylo)[b]], rx.at[g, d, b], all_x[d], (yl, ylo)[b])

        def over_yl():
            return rr(7, tf.at[g], ryl.at[g], x, ylo)

        def own_sum(ax, ayl):
            return acc[p, g, ax * 2 + ayl, core] + rd[g, ax * 2 + ayl]

        if step == 0:
            over_core().start()
        if step == 1:
            over_core().wait()
            if direct:
                tf[g] = bf16(own_sum(x, ylo))
                over_yl().start()
            for d in (2, 0, 1):
                for b in range(2):
                    rq[g, all_x[d], b] = bf16(own_sum(all_x[d], b))
                if direct:
                    for b in range(2):
                        over_x(d, b).start()
                else:
                    over_x(d).start()
        if step == 2 and not direct:
            for d in range(3):
                over_x(d).wait()
            tf[g] = bf16(own_sum(x, ylo) + f32(rx[g, 0, ylo]) + f32(rx[g, 1, ylo]) + f32(rx[g, 2, ylo]))
            over_yl().start()
        if step == 3:
            total = own_sum(x, yl)
            for d in range(3):
                if direct:
                    for b in range(2):
                        over_x(d, b).wait()
                        total = total + f32(rx[g, d, b])
                else:
                    total = total + f32(rx[g, d, yl])
            over_yl().wait()
            total = bf16(total + f32(ryl[g]))
            rows = pl.ds(pl.multiple_of(g * GR, GR), GR)

            @pl.when(p == 0)
            def _():
                out_ref[rows, :] = total

            @pl.when(p == 1)
            def _():
                ig_ref[rows, :] = total

    def rs_unit(t):
        late = t - NN
        u = jnp.where(t < NN, t, NN + late // 2)
        return u, (t >= 0) & (t < 3 * NN) & ((t < NN) | (late % 2 == 0))

    def ag_unit(t):
        early = t - AG1
        u = jnp.where(t < AG2, early // 2, NN + t - AG2)
        return u, ((t >= AG1) & (t < AG2) & (early % 2 == 0)) | ((t >= AG2) & (t < AG2 + NN))

    def at_ticks(steps):
        def find(t):
            n, ok = jnp.int32(0), jnp.bool_(False)
            for e, at in steps:
                n = n + jnp.where(t == at, e, 0)
                ok = ok | (t == at)
            return n, ok

        return find

    gathers = [
        (1, (None, None, 0, 2, 4)),
        (2, (None, 2, 4, 6, 8)),
        (3, (1, 4, 7, 9, 12)),
        (4, (7, 10, 13, 16, 19)),
        (5, (13, 16, 19, 22, 25)),
    ]
    scatters = [(g, AG1 + 2 * (NC * g + NC - 1) + A4 + 1) for g in range(NG)]
    scatters += [(NG + g, AG2 + NC * g + NC - 1 + A4 + 1) for g in range(NG - 1)]
    scatters = [(e, tuple(start + 2 * k for k in range(4))) for e, start in scatters]

    def tick(t, carry):
        def run(offset, unit_of, fn):
            u, ok = unit_of(t - offset)

            @pl.when(ok)
            def _():
                fn(u)

        run(A4, ag_unit, gather4)
        run(A3, ag_unit, gather3)
        run(A2, ag_unit, gather2)
        run(S4, rs_unit, stage4)
        run(0, ag_unit, gather1)
        run(S3, rs_unit, stage3)
        run(S2, rs_unit, stage2)
        for step in range(4, -1, -1):
            run(0, at_ticks([(e, ticks[step]) for e, ticks in gathers if ticks[step] is not None]),
                lambda e, step=step: gather_step(e // NG, e % NG, step))
        for step in range(3, -1, -1):
            run(0, at_ticks([(e, ticks[step]) for e, ticks in scatters if ticks[step] < TICKS]),
                lambda e, step=step: scatter_step(e // NG, e % NG, step))
        run(0, rs_unit, product)
        run(A4, ag_unit, use)

        @pl.when(t == 28)
        def _():
            for c in range(12):
                cblk[c] = panel[1, :, :, :, c * BLK : (c + 1) * BLK].reshape(16 * OWN, BLK)

        @pl.when(t == 30)
        def _():
            xt[...] = panel[0].reshape(16 * OWN, DW).T

        @pl.when((t >= SG) & (t < SG + 12))
        def _():
            second(2 * (t - SG))
            second(2 * (t - SG) + 1)

        return carry

    lax.fori_loop(0, TICKS, tick, 0)
    scatter_step(1, NG - 1, 0, direct=True)
    for e, ticks in scatters:
        for step in range(4):
            if ticks[step] >= TICKS:
                scatter_step(e // NG, e % NG, step)
    first(0)
    scatter_step(1, NG - 1, 1, direct=True)
    for i in range(1, 12):
        first(i)
    scatter_step(1, NG - 1, 3, direct=True)
    for i in range(2):
        second_out(22 + i).wait()
        first_out(10 + i).wait()


def shards(inputs, first_values, first_blocks, second_values, second_blocks, cotangent):
    pick1 = first_blocks - lax.axis_index("row") * 24
    pick2 = second_blocks - lax.axis_index("col") * 12

    def slot_table(pick, width):
        rows, slots = pick.shape
        number = jnp.arange(rows * slots, dtype=jnp.int32).reshape(rows, slots) - rows * slots
        hit = pick[:, :, None] == jnp.arange(width, dtype=jnp.int32)
        return rows * slots + jnp.sum(jnp.where(hit, number[:, :, None], 0), axis=1)

    inv1 = slot_table(pick1, 24)
    inv2 = slot_table(pick2, 12)
    bf, fl = jnp.bfloat16, jnp.float32
    smem = pl.BlockSpec(memory_space=pltpu.SMEM)
    vmem = pl.BlockSpec(memory_space=pltpu.VMEM)
    dma = pltpu.SemaphoreType.DMA
    v1 = first_values.reshape(72, BLK, BLK)
    v2 = second_values.reshape(72, BLK, BLK)
    return pl.pallas_call(
        kernel,
        out_shape=(
            jax.ShapeDtypeStruct((OWN, DW), bf),
            jax.ShapeDtypeStruct((OWN, DW), bf),
            jax.ShapeDtypeStruct((12, 6, BLK, BLK), bf),
            jax.ShapeDtypeStruct((24, 3, BLK, BLK), bf),
        ),
        in_specs=[smem] * 4 + [vmem] * 2 + [pl.BlockSpec(memory_space=pl.ANY)] * 2,
        out_specs=(vmem,) * 2 + (pl.BlockSpec(memory_space=pl.ANY),) * 2,
        scratch_shapes=[
            pltpu.VMEM((2, NG, 16, GR, DW), bf),
            pltpu.VMEM((12, 16 * OWN, BLK), bf),
            pltpu.VMEM((DW, 16 * OWN), bf),
            pltpu.VMEM((73, BLK, BLK), bf),
            pltpu.VMEM((73, BLK, BLK), bf),
            pltpu.VMEM((DW, CW), bf),
            pltpu.VMEM((CW, DW), bf),
            pltpu.VMEM((NP, 4, 2, SR, CW), fl),
            pltpu.VMEM((NT, 4, GR, CW), bf),
            pltpu.VMEM((NT, 2, GR, CW // 2), bf),
            pltpu.VMEM((NT, 2, GR, CW), bf),
            pltpu.VMEM((NT, 2, 2, GR, CW // 2), bf),
            pltpu.VMEM((NT, 2, 2, GR, CW), bf),
            pltpu.VMEM((NT, GR, CW), bf),
            pltpu.VMEM((NS, 4, GR, CW), bf),
            pltpu.VMEM((NS, 2, GR, CW // 2), bf),
            pltpu.VMEM((NS, 2, GR, CW), bf),
            pltpu.VMEM((NS, 2, 2, GR, CW // 2), bf),
            pltpu.VMEM((NS, 2, 2, GR, CW), bf),
            pltpu.VMEM((NS, GR, CW), bf),
            pltpu.VMEM((2, NC * CB, NG, 4, 2, SR, BLK), bf),
            pltpu.VMEM((NN, SR, CW), fl),
            pltpu.VMEM((2, NG, 8, 2, GR, DW), fl),
            pltpu.VMEM((NG, 8, GR, DW), fl),
            pltpu.VMEM((NG, 4, 2, GR, DW), bf),
            pltpu.VMEM((NG, 3, 2, GR, DW), bf),
            pltpu.VMEM((NG, GR, DW), bf),
            pltpu.VMEM((NG, GR, DW), bf),
            pltpu.VMEM((2, 3, BLK, BLK), bf),
            pltpu.VMEM((2, 6, BLK, BLK), bf),
            dma((6,)),
            dma((NS, 10)), dma((NS, 10)), dma((NA, 10)), dma((NA, 10)),
            dma((2, NG, 15)), dma((2, NG, 15)), dma((2 * NG, 8)), dma((2 * NG, 8)),
        ],
        compiler_params=pltpu.CompilerParams(
            collective_id=1, has_side_effects=True, vmem_limit_bytes=62 * 2**20
        ),
        name="sparse_ffn",
    )(inv1, inv2, pick1, pick2, inputs, cotangent, v1, v2)


def solution(mesh):
    placed = (
        P("row", "col"),
        P("col", "row", None, None),
        P("col", "row"),
        P("row", "col", None, None),
        P("row", "col"),
        P("row", "col"),
    )
    return jax.shard_map(
        shards,
        mesh=mesh,
        in_specs=placed,
        out_specs=(
            P("row", "col"),
            P("row", "col"),
            P("col", "row", None, None),
            P("row", "col", None, None),
        ),
        check_vma=False,
    )
```

```python
import jax
import jax.numpy as jnp
from jax import lax
from jax.experimental import pallas as pl
from jax.experimental.pallas import tpu as pltpu
from jax.sharding import PartitionSpec as P

MESH = pl.DeviceIdType.MESH
gelu_scale = 0.7978845608028654
gelu_cubic = 0.044715

BLK = 128
NG = 3
NC = 4
CB = 6
CW = CB * BLK
YB = 2
AB = 4
YW, ZW = YB * BLK, (CB - YB) * BLK
NN = NG * NC
NU = 2 * NN
NS = 12
NR = 7
NT = 3
NP = 9
GR = 16
SR = 2 * GR
OWN = NG * GR
DW = 1536
S2, S3, S4 = 3, 6, 9
A2, A3, A4 = 3, 6, 9
AG1, AG2 = NN + 1, 3 * NN
TICKS = AG2 + NN + A4
SG = AG1 + 2 * NN + A4 - 1


def gelu_pair(pre_act):
    inner_arg = gelu_scale * (pre_act + gelu_cubic * pre_act * pre_act * pre_act)
    tanh_value = jnp.tanh(inner_arg)
    activated = 0.5 * pre_act * (1.0 + tanh_value)
    derivative = 0.5 * (1.0 + tanh_value) + 0.5 * pre_act * (
        1.0 - tanh_value * tanh_value
    ) * gelu_scale * (1.0 + 3.0 * gelu_cubic * pre_act * pre_act)
    return (activated, derivative)


def f32(v):
    return v.astype(jnp.float32)


def bf16(v):
    return v.astype(jnp.bfloat16)


def dot(a, b, ca, cb):
    return lax.dot_general(a, b, (((ca,), (cb,)), ((), ())), preferred_element_type=jnp.float32)


def kernel(
    blocks1, blocks2, x_in, c_in, v1_hbm, v2_hbm,
    out_ref, ig_ref, fg_ref, sg_ref,
    panel, cblk, xt, v1, v2, wd1, wd2, part, sy_y, szo_y, sz_y, szo_z, sz_z, sy_z,
    ry_y, rzo_y, rz_y, rzo_z, rz_z, ry_z,
    gath, deriv, acc, rd, rq, rx, ryl, tf, sgb, fgb, inv1, inv2,
    v_sem, rs_s, rs_r, ag_s, ag_r, rg_s, rg_r, rr_s, rr_r,
):
    row, col = lax.axis_index("row"), lax.axis_index("col")
    x, yl, core = row // 4, (row // 2) % 2, row % 2
    z, y = col // 2, col % 2
    zp, zm, zo = (z + 1) % 4, (z + 3) % 4, (z + 2) % 4
    xp, xm, xo = (x + 1) % 4, (x + 3) % 4, (x + 2) % 4
    yo, ylo, co = 1 - y, 1 - yl, 1 - core

    def at_row(ax, ayl, ac):
        return (ax * 2 + ayl) * 2 + ac

    dev_z = ((row, zp * 2 + y), (row, zm * 2 + y))
    dev_y = (row, z * 2 + yo)
    dev_row = [(at_row(ax, yl, core), col) for ax in (xp, xm, xo)]
    dev_row += [(at_row(ax, ylo, core), col) for ax in (x, xp, xm, xo)]
    dev_row += [(at_row(x, yl, co), col)]

    barrier = pltpu.get_barrier_semaphore()
    for dev in (*dev_z, dev_y, *dev_row):
        pl.semaphore_signal(barrier, inc=1, device_id=dev, device_id_type=MESH)

    def copy(src, dst, send, recv, dev):
        return pltpu.make_async_remote_copy(
            src_ref=src, dst_ref=dst, send_sem=send, recv_sem=recv, device_id=dev, device_id_type=MESH
        )

    load1 = pltpu.make_async_copy(v1_hbm, v1.at[pl.ds(0, 72)], v_sem.at[0])
    load2 = pltpu.make_async_copy(v2_hbm, v2.at[pl.ds(0, 72)], v_sem.at[1])
    load1.start()
    load2.start()
    for g in range(NG):
        panel[0, g, row // 2, core] = x_in[pl.ds(g * GR, GR)]
        panel[1, g, row // 2, core] = c_in[pl.ds(g * GR, GR)]
    pl.semaphore_wait(barrier, 11)


    order = [(x, yl), (x, ylo), (xp, yl), (xm, yl), (xo, yl), (xp, ylo), (xm, ylo), (xo, ylo)]
    all_x = (xp, xm, xo)
    from_x = (xm, xp, xo)

    def gather_step(p, g, step, direct=False):
        def rg(k, src, ax, ayl):
            return copy(src, src, rg_s.at[p, g, 0], rg_r.at[p, g, k], (at_row(ax, ayl, core), col))

        def piece(ax, ayl):
            return panel.at[p, g, ax * 2 + ayl, core]

        def over_yl(side):
            return rg(0, piece(x, side), x, ylo)

        def own_x(d, at):
            return rg(1 + d, piece(at, yl), all_x[d], yl)

        def other_x(d, at):
            if direct:
                return rg(4 + d, piece(at, ylo if at is not x else yl), all_x[d], ylo)
            return rg(4 + d, piece(at, ylo), all_x[d], yl)

        def core_copy(src):
            return copy(src, src, rg_s.at[p, g, 1], rg_r.at[p, g, 7], (at_row(x, yl, co), col))

        def to_core(i):
            return core_copy(piece(*order[i]))

        if step == 0:
            over_yl(yl).start()
            for d in range(3):
                own_x(d, x).start()
            if direct:
                for d in range(3):
                    other_x(d, x).start()
            to_core(0).start()
        if step == 1:
            over_yl(ylo).wait_recv()
            if not direct:
                for d in range(3):
                    other_x(d, x).start()
            to_core(1).start()
        if step == 2:
            for d in range(3):
                own_x(d, from_x[d]).wait_recv()
                to_core(2 + (1, 0, 2)[d]).start()
        if step == 3:
            for d in range(3):
                other_x(d, from_x[d]).wait_recv()
                to_core(5 + (1, 0, 2)[d]).start()
        if step == 4:
            rg(0, panel.at[p, g, pl.ds(0, 7), core], x, ylo).wait_send()
            core_copy(panel.at[p, g, :, core]).wait_send()
            core_copy(panel.at[p, g, :, co]).wait_recv()

    def slot_table(table, blocks, base, rows, width, slots):
        def fill(i, carry):
            names = [blocks[k, i] - base for k in range(slots)]
            for h in range(width):
                found = jnp.int32(rows * slots)
                for k in range(slots):
                    found = jnp.where(names[k] == h, i * slots + k, found)
                table[i, h] = found
            return carry

        lax.fori_loop(0, rows, fill, 0)

    for step in range(5):
        gather_step(0, 0, step, direct=True)
        if step == 0:
            v1[72] = jnp.zeros((BLK, BLK), jnp.bfloat16)
            v2[72] = jnp.zeros((BLK, BLK), jnp.bfloat16)
            acc[...] = jnp.zeros(acc.shape, jnp.float32)
            slot_table(inv1, blocks1, row * 24, 12, 24, 6)
            slot_table(inv2, blocks2, col * 12, 24, 12, 3)
        if step == 1:
            gather_step(0, 1, 0)
        if step == 3:
            gather_step(0, 1, 1)
            gather_step(0, 2, 0)
    load1.wait()
    load2.wait()

    def dense1(c):
        for i in range(12):
            for h in range(CB):
                wd1[pl.ds(i * BLK, BLK), pl.ds(h * BLK, BLK)] = v1[inv1[i, c * CB + h]]
        return wd1[...]

    def dense2(c):
        for h in range(CB):
            for i in range(12):
                wd2[pl.ds(h * BLK, BLK), pl.ds(i * BLK, BLK)] = v2[inv2[c * CB + h, i]]
        return wd2[...]

    yw, zw = pl.ds(0, YW), pl.ds(YW, ZW)
    yh = (pl.ds(0, YW // 2), pl.ds(YW // 2, YW // 2))
    zh = (pl.ds(YW, ZW // 2), pl.ds(YW + ZW // 2, ZW // 2))
    tgt, src_z = (zp, zm), (zm, zp)

    def rs(u, k, src, dst, dev):
        return copy(src, dst, rs_s.at[u % NT, k], rs_r.at[u % NR, k], dev)

    def rs_y_y(u):
        return rs(u, 0, sy_y.at[u % NT], ry_y.at[u % NS], dev_y)

    def rs_zo_y(u, d):
        return rs(u, 1 + d, szo_y.at[u % NT, d], rzo_y.at[u % NS, d], dev_z[d])

    def rs_z_y(u, d):
        return rs(u, 3 + d, sz_y.at[u % NT, d], rz_y.at[u % NS, d], dev_z[d])

    def rs_zo_z(u, d):
        return rs(u, 5 + d, szo_z.at[u % NT, d], rzo_z.at[u % NS, d], dev_z[d])

    def rs_z_z(u, d):
        return rs(u, 7 + d, sz_z.at[u % NT, d], rz_z.at[u % NS, d], dev_z[d])

    def rs_y_z(u):
        return rs(u, 9, sy_z.at[u % NT], ry_z.at[u % NS], dev_y)

    def product(u):
        sp, s2 = u % NP, u % NT
        g, c = (u // NC) % NG, u % NC

        @pl.when(u < NN)
        def _():
            r = dot(panel[0, g].reshape(16 * GR, DW), dense1(c), 1, 0)
            part[sp] = r.reshape(4, 2, SR, CW)

        @pl.when(u >= NN)
        def _():
            r = dot(panel[1, g].reshape(16 * GR, DW), dense2(c), 1, 1)
            part[sp] = r.reshape(4, 2, SR, CW)

        sy_y[s2] = bf16(part[sp, :, yo, :, yw])
        rs_y_y(u).start()
        for d in range(2):
            szo_z[s2, d] = bf16(part[sp, zo, :, :, zh[d]])
            rs_zo_z(u, d).start()

    def stage2(u):
        s, sp, s2 = u % NS, u % NP, u % NT
        rs_y_y(u).wait()
        for d in range(2):
            szo_y[s2, d] = bf16(part[sp, zo, y, :, yh[d]] + f32(ry_y[s, zo, :, yh[d]]))
            rs_zo_y(u, d).start()
        for d in range(2):
            rs_zo_z(u, d).wait()
            for e in range(2):
                total = part[sp, tgt[d], :, :, zh[e]]
                if e == d:
                    total = total + f32(rzo_z[s, d])
                sz_z[s2, d, :, :, pl.ds(e * (ZW // 2), ZW // 2)] = bf16(total)
            rs_z_z(u, d).start()

    def stage3(u):
        s, sp, s2 = u % NS, u % NP, u % NT
        for d in range(2):
            rs_zo_y(u, d).wait()
            for e in range(2):
                total = part[sp, tgt[d], y, :, yh[e]] + f32(ry_y[s, tgt[d], :, yh[e]])
                if e == d:
                    total = total + f32(rzo_y[s, d])
                sz_y[s2, d, :, yh[e]] = bf16(total)
            rs_z_y(u, d).start()
        for d in range(2):
            rs_z_z(u, d).wait()
        sy_z[s2] = bf16(part[sp, z, yo, :, zw] + f32(rz_z[s, 0, yo]) + f32(rz_z[s, 1, yo]))
        rs_y_z(u).start()

    def stage4(u):
        s, sp = u % NS, u % NP
        g, c = (u // NC) % NG, u % NC
        for d in range(2):
            rs_z_y(u, d).wait()
        sum_y = part[sp, z, y, :, yw] + f32(ry_y[s, z]) + f32(rz_y[s, 0]) + f32(rz_y[s, 1])
        rs_y_z(u).wait()
        sum_z = part[sp, z, y, :, zw] + f32(rz_z[s, 0, y]) + f32(rz_z[s, 1, y]) + f32(ry_z[s])

        def keep(p, first_block, value):
            for b in range(value.shape[1] // BLK):
                gath[p, c * CB + first_block + b, g, z, y] = bf16(value[:, b * BLK : (b + 1) * BLK])

        @pl.when(u < NN)
        def _():
            for lo, cols, total in ((0, yw, sum_y), (YB, zw, sum_z)):
                activated, derivative = gelu_pair(total)
                keep(0, lo, activated)
                deriv[u, :, cols] = derivative

        @pl.when(u >= NN)
        def _():
            for lo, cols, total in ((0, yw, sum_y), (YB, zw, sum_z)):
                keep(1, lo, total * deriv[u - NN, :, cols])

    def ag_of(u, p):
        g, c = (u // NC) % NG, u % NC

        def part_of(first_block, blocks, first_row, rows):
            return lambda at, side: gath.at[
                p, pl.ds(c * CB + first_block, blocks), g, at, side, pl.ds(first_row, rows)
            ]

        if p == 0:
            yb, zb = part_of(0, CB, 0, GR), part_of(0, CB, GR, GR)
            yhalf = [part_of(d * CB // 2, CB // 2, 0, GR) for d in range(2)]
            zhalf = [part_of(d * CB // 2, CB // 2, GR, GR) for d in range(2)]
        else:
            zb_n = CB - AB
            yb, zb = part_of(0, AB, 0, SR), part_of(AB, zb_n, 0, SR)
            yhalf = [part_of(d * AB // 2, AB // 2, 0, SR) for d in range(2)]
            zhalf = [part_of(AB + d * zb_n // 2, zb_n // 2, 0, SR) for d in range(2)]
        every = slice(None)

        def ag(k, ref, dev):
            return copy(ref, ref, ag_s.at[u % NT, k], ag_r.at[u % NR, k], dev)

        return (
            lambda side: ag(0, yb(z, side), dev_y),
            lambda d, at: ag(1 + d, yb(at, every), dev_z[d]),
            lambda d, at: ag(3 + d, yhalf[d](at, every), dev_z[d]),
            lambda d, at: ag(5 + d, zb(at, y), dev_z[d]),
            lambda d, at: ag(7 + d, zhalf[d](at, y), dev_z[d]),
            lambda side: ag(9, zb(every, side), dev_y),
        )

    def either(fn):
        def run(u):
            for p in range(2):
                @pl.when(u // NN == p)
                def _():
                    fn(*ag_of(u, p))

        return run

    @either
    def gather1(y_y, z_y, zo_y, z_z, zo_z, y_z):
        y_y(y).start()
        for d in range(2):
            z_z(d, z).start()

    @either
    def gather2(y_y, z_y, zo_y, z_z, zo_z, y_z):
        y_y(yo).wait_recv()
        for d in range(2):
            z_y(d, z).start()
        for d in range(2):
            z_z(d, src_z[d]).wait_recv()
            zo_z(d, src_z[d]).start()
        y_y(y).wait_send()
        for d in range(2):
            z_z(d, z).wait_send()

    @either
    def gather3(y_y, z_y, zo_y, z_z, zo_z, y_z):
        for d in range(2):
            z_y(d, src_z[d]).wait_recv()
            zo_y(d, src_z[d]).start()
        for d in range(2):
            zo_z(d, zo).wait_recv()
        y_z(y).start()
        for d in range(2):
            z_y(d, z).wait_send()
            zo_z(d, src_z[d]).wait_send()

    @either
    def gather4(y_y, z_y, zo_y, z_z, zo_z, y_z):
        for d in range(2):
            zo_y(d, zo).wait_recv()
        y_z(yo).wait_recv()
        y_z(y).wait_send()
        for d in range(2):
            zo_y(d, src_z[d]).wait_send()

    def use(u):
        p, g, c = u // NN, (u // NC) % NG, u % NC
        rows = jnp.concatenate([gath[p, c * CB + b, g].reshape(16 * GR, BLK) for b in range(CB)], axis=1)

        @pl.when(p == 0)
        def _():
            acc[0, g] += dot(rows, dense2(c), 1, 0).reshape(8, 2, GR, DW)

        @pl.when(p == 1)
        def _():
            acc[1, g] += dot(rows, dense1(c), 1, 1).reshape(8, 2, GR, DW)

    def local_block(blocks, i, k, base, width):
        return jnp.clip(blocks[k, i] - base, 0, width - 1)

    def second_out(j):
        return pltpu.make_async_copy(sgb.at[j % 2], sg_ref.at[j], v_sem.at[2 + j % 2])

    def second(j):
        flipped = gath[0, j].reshape(16 * OWN, BLK).T
        picked = jnp.concatenate([cblk[local_block(blocks2, j, k, col * 12, 12)] for k in range(3)], axis=1)
        g = bf16(dot(flipped, picked, 1, 0))

        @pl.when(j >= 2)
        def _():
            second_out(j - 2).wait()

        for k in range(3):
            sgb[j % 2, k] = g[:, k * BLK : (k + 1) * BLK]
        second_out(j).start()

    def first_out(i):
        return pltpu.make_async_copy(fgb.at[i % 2], fg_ref.at[i], v_sem.at[4 + i % 2])

    def first(i):
        picked = jnp.concatenate([gath[1, local_block(blocks1, i, k, row * 24, 24)].reshape(16 * OWN, BLK) for k in range(6)], axis=1)
        g = bf16(dot(xt[pl.ds(i * BLK, BLK), :], picked, 1, 0))
        if i >= 2:
            first_out(i - 2).wait()
        for k in range(6):
            fgb[i % 2, k] = g[:, k * BLK : (k + 1) * BLK]
        first_out(i).start()

    def scatter_step(p, g, step, direct=False):
        e = p * NG + g

        def rr(k, src, dst, ax, ayl, ac=core):
            send = rr_s.at[e, 0 if k == 0 else 2 if k == 7 else 1]
            return copy(src, dst, send, rr_r.at[e, k], (at_row(ax, ayl, ac), col))

        def over_core():
            return rr(0, acc.at[p, g, :, co], rd.at[g], x, yl, co)

        def over_x(d, b=None):
            if b is None:
                return rr(1 + d, rq.at[g, all_x[d]], rx.at[g, d], all_x[d], yl)
            return rr(1 + 2 * d + b, rq.at[g, all_x[d], (yl, ylo)[b]], rx.at[g, d, b], all_x[d], (yl, ylo)[b])

        def over_yl():
            return rr(7, tf.at[g], ryl.at[g], x, ylo)

        def sent():
            rr(1, rq.at[g, pl.ds(0, 3)], rx.at[g], xp, yl).wait_send()

        def own_sum(ax, ayl):
            return acc[p, g, ax * 2 + ayl, core] + rd[g, ax * 2 + ayl]

        if step == 0:
            over_core().start()
        if step == 1:
            over_core().wait()
            if direct:
                tf[g] = bf16(own_sum(x, ylo))
                over_yl().start()
            for d in (2, 0, 1):
                for b in range(2):
                    rq[g, all_x[d], b] = bf16(own_sum(all_x[d], b))
                if direct:
                    for b in range(2):
                        over_x(d, b).start()
                else:
                    over_x(d).start()
        if step == 2 and not direct:
            for d in range(3):
                over_x(d).wait_recv()
            sent()
            tf[g] = bf16(own_sum(x, ylo) + f32(rx[g, 0, ylo]) + f32(rx[g, 1, ylo]) + f32(rx[g, 2, ylo]))
            over_yl().start()
        if step == 3:
            total = own_sum(x, yl)
            for d in range(3):
                if direct:
                    for b in range(2):
                        over_x(d, b).wait_recv()
                        total = total + f32(rx[g, d, b])
                else:
                    total = total + f32(rx[g, d, yl])
            if direct:
                sent()
            over_yl().wait()
            total = bf16(total + f32(ryl[g]))
            rows = pl.ds(pl.multiple_of(g * GR, GR), GR)

            @pl.when(p == 0)
            def _():
                out_ref[rows, :] = total

            @pl.when(p == 1)
            def _():
                ig_ref[rows, :] = total

    def rs_unit(t):
        late = t - NN
        u = jnp.where(t < NN, t, NN + late // 2)
        return u, (t >= 0) & (t < 3 * NN) & ((t < NN) | (late % 2 == 0))

    def ag_unit(t):
        early = t - AG1
        u = jnp.where(t < AG2, early // 2, NN + t - AG2)
        return u, ((t >= AG1) & (t < AG2) & (early % 2 == 0)) | ((t >= AG2) & (t < AG2 + NN))

    def at_ticks(steps):
        def find(t):
            n, ok = jnp.int32(0), jnp.bool_(False)
            for e, at in steps:
                n = n + jnp.where(t == at, e, 0)
                ok = ok | (t == at)
            return n, ok

        return find

    gathers = [
        (1, (None, None, 0, 2, 4)),
        (2, (None, 2, 4, 6, 8)),
        (3, (1, 4, 7, 9, 12)),
        (4, (7, 10, 13, 16, 19)),
        (5, (13, 16, 19, 22, 25)),
    ]
    scatters = [(g, AG1 + 2 * (NC * g + NC - 1) + A4 + 1) for g in range(NG)]
    scatters += [(NG + g, AG2 + NC * g + NC - 1 + A4 + 1) for g in range(NG - 1)]
    scatters = [(e, tuple(start + 2 * k for k in range(4))) for e, start in scatters]

    def tick(t, carry):
        def run(offset, unit_of, fn):
            u, ok = unit_of(t - offset)

            @pl.when(ok)
            def _():
                fn(u)

        run(A4, ag_unit, gather4)
        run(A3, ag_unit, gather3)
        run(A2, ag_unit, gather2)
        run(S4, rs_unit, stage4)
        run(0, ag_unit, gather1)
        run(S3, rs_unit, stage3)
        run(S2, rs_unit, stage2)
        for step in range(4, -1, -1):
            run(0, at_ticks([(e, ticks[step]) for e, ticks in gathers if ticks[step] is not None]),
                lambda e, step=step: gather_step(e // NG, e % NG, step))
        for step in range(3, -1, -1):
            run(0, at_ticks([(e, ticks[step]) for e, ticks in scatters if ticks[step] < TICKS]),
                lambda e, step=step: scatter_step(e // NG, e % NG, step))
        run(0, rs_unit, product)
        run(A4, ag_unit, use)

        @pl.when(t == 28)
        def _():
            for c in range(12):
                cblk[c] = panel[1, :, :, :, :, c * BLK : (c + 1) * BLK].reshape(16 * OWN, BLK)

        @pl.when(t == 30)
        def _():
            xt[...] = panel[0].reshape(16 * OWN, DW).T

        @pl.when((t >= SG) & (t < SG + 12))
        def _():
            second(2 * (t - SG))
            second(2 * (t - SG) + 1)

        return carry

    lax.fori_loop(0, TICKS, tick, 0)
    scatter_step(1, NG - 1, 0, direct=True)
    for e, ticks in scatters:
        for step in range(4):
            if ticks[step] >= TICKS:
                scatter_step(e // NG, e % NG, step)
    first(0)
    scatter_step(1, NG - 1, 1, direct=True)
    for i in range(1, 12):
        first(i)
    scatter_step(1, NG - 1, 3, direct=True)
    for i in range(2):
        second_out(22 + i).wait()
        first_out(10 + i).wait()


def hand_over(*refs):
    ins, outs, bufs, (sem_in, sem_out) = refs[:4], refs[4:8], refs[8:12], refs[12:]
    loads, stores = [], []
    for src, dst, buf in zip(ins, outs, bufs):
        pieces = 6 if len(src.shape) == 4 else 1
        size = src.shape[0] // pieces
        for k in range(pieces):
            rows = pl.ds(k * size, size)
            n = len(loads)
            loads.append(pltpu.make_async_copy(src.at[rows], buf.at[rows], sem_in.at[n]))
            stores.append(pltpu.make_async_copy(buf.at[rows], dst.at[rows], sem_out.at[n]))
    for load in loads:
        load.start()
    for load, store in zip(loads, stores):
        load.wait()
        store.start()
    for store in stores:
        store.wait()


def shards(inputs, first_values, first_blocks, second_values, second_blocks, cotangent):
    bf, fl = jnp.bfloat16, jnp.float32
    smem = pl.BlockSpec(memory_space=pltpu.SMEM)
    vmem = pl.BlockSpec(memory_space=pltpu.VMEM)
    dma = pltpu.SemaphoreType.DMA
    v1 = first_values.reshape(72, BLK, BLK)
    v2 = second_values.reshape(72, BLK, BLK)
    results = pl.pallas_call(
        kernel,
        out_shape=(
            jax.ShapeDtypeStruct((OWN, DW), bf),
            jax.ShapeDtypeStruct((OWN, DW), bf),
            jax.ShapeDtypeStruct((12, 6, BLK, BLK), bf),
            jax.ShapeDtypeStruct((24, 3, BLK, BLK), bf),
        ),
        in_specs=[smem] * 2 + [vmem] * 2 + [pl.BlockSpec(memory_space=pl.ANY)] * 2,
        out_specs=(vmem,) * 2 + (pl.BlockSpec(memory_space=pl.ANY),) * 2,
        scratch_shapes=[
            pltpu.VMEM((2, NG, 8, 2, GR, DW), bf),
            pltpu.VMEM((12, 16 * OWN, BLK), bf),
            pltpu.VMEM((DW, 16 * OWN), bf),
            pltpu.VMEM((73, BLK, BLK), bf),
            pltpu.VMEM((73, BLK, BLK), bf),
            pltpu.VMEM((DW, CW), bf),
            pltpu.VMEM((CW, DW), bf),
            pltpu.VMEM((NP, 4, 2, SR, CW), fl),
            pltpu.VMEM((NT, 4, SR, YW), bf),
            pltpu.VMEM((NT, 2, SR, YW // 2), bf),
            pltpu.VMEM((NT, 2, SR, YW), bf),
            pltpu.VMEM((NT, 2, 2, SR, ZW // 2), bf),
            pltpu.VMEM((NT, 2, 2, SR, ZW), bf),
            pltpu.VMEM((NT, SR, ZW), bf),
            pltpu.VMEM((NS, 4, SR, YW), bf),
            pltpu.VMEM((NS, 2, SR, YW // 2), bf),
            pltpu.VMEM((NS, 2, SR, YW), bf),
            pltpu.VMEM((NS, 2, 2, SR, ZW // 2), bf),
            pltpu.VMEM((NS, 2, 2, SR, ZW), bf),
            pltpu.VMEM((NS, SR, ZW), bf),
            pltpu.VMEM((2, NC * CB, NG, 4, 2, SR, BLK), bf),
            pltpu.VMEM((NN, SR, CW), fl),
            pltpu.VMEM((2, NG, 8, 2, GR, DW), fl),
            pltpu.VMEM((NG, 8, GR, DW), fl),
            pltpu.VMEM((NG, 4, 2, GR, DW), bf),
            pltpu.VMEM((NG, 3, 2, GR, DW), bf),
            pltpu.VMEM((NG, GR, DW), bf),
            pltpu.VMEM((NG, GR, DW), bf),
            pltpu.VMEM((2, 3, BLK, BLK), bf),
            pltpu.VMEM((2, 6, BLK, BLK), bf),
            pltpu.SMEM((12, 24), jnp.int32),
            pltpu.SMEM((24, 12), jnp.int32),
            dma((6,)),
            dma((NT, 10)), dma((NR, 10)), dma((NT, 10)), dma((NR, 10)),
            dma((2, NG, 2)), dma((2, NG, 8)), dma((2 * NG, 3)), dma((2 * NG, 8)),
        ],
        compiler_params=pltpu.CompilerParams(
            collective_id=1, has_side_effects=True, vmem_limit_bytes=62 * 2**20
        ),
        name="sparse_ffn",
    )(first_blocks.T, second_blocks.T, inputs, cotangent, v1, v2)
    anywhere = pl.BlockSpec(memory_space=pl.ANY)
    return pl.pallas_call(
        hand_over,
        out_shape=tuple(jax.ShapeDtypeStruct(r.shape, r.dtype) for r in results),
        in_specs=[anywhere] * 4,
        out_specs=(anywhere,) * 4,
        scratch_shapes=[pltpu.VMEM(r.shape, r.dtype) for r in results] + [dma((14,)), dma((14,))],
        name="hand_over",
    )(*results)


def solution(mesh):
    placed = (
        P("row", "col"),
        P("col", "row", None, None),
        P("col", "row"),
        P("row", "col", None, None),
        P("row", "col"),
        P("row", "col"),
    )
    return jax.shard_map(
        shards,
        mesh=mesh,
        in_specs=placed,
        out_specs=(
            P("row", "col"),
            P("row", "col"),
            P("col", "row", None, None),
            P("row", "col", None, None),
        ),
        check_vma=False,
    )
```

```python
import jax
import jax.numpy as jnp
from jax import lax
from jax.experimental import pallas as pl
from jax.experimental.pallas import tpu as pltpu
from jax.sharding import PartitionSpec as P

MESH = pl.DeviceIdType.MESH
gelu_scale = 0.7978845608028654
gelu_cubic = 0.044715

BLK = 128
NG = 3
NC = 4
CB = 6
CW = CB * BLK
YB = 2
AB = 4
YW, ZW = YB * BLK, (CB - YB) * BLK
NN = NG * NC
NU = 2 * NN
NS = 12
NR = 7
NT = 3
NP = 9
GR = 16
SR = 2 * GR
OWN = NG * GR
DW = 1536
S2, S3, S4 = 3, 6, 9
A2, A3, A4 = 3, 6, 9
AG1, AG2 = NN + 1, 3 * NN
TICKS = AG2 + NN + A4
SG = AG1 + 2 * NN + A4 - 1


def gelu_pair(pre_act):
    inner_arg = gelu_scale * (pre_act + gelu_cubic * pre_act * pre_act * pre_act)
    tanh_value = jnp.tanh(inner_arg)
    activated = 0.5 * pre_act * (1.0 + tanh_value)
    derivative = 0.5 * (1.0 + tanh_value) + 0.5 * pre_act * (
        1.0 - tanh_value * tanh_value
    ) * gelu_scale * (1.0 + 3.0 * gelu_cubic * pre_act * pre_act)
    return (activated, derivative)


def f32(v):
    return v.astype(jnp.float32)


def bf16(v):
    return v.astype(jnp.bfloat16)


def dot(a, b, ca, cb):
    return lax.dot_general(a, b, (((ca,), (cb,)), ((), ())), preferred_element_type=jnp.float32)


def kernel(
    blocks1, blocks2, x_in, c_in, v1_hbm, v2_hbm,
    out_ref, ig_ref, fg_ref, sg_ref,
    panel, cblk, xt, v1, v2, wd1, wd2, part, sy_y, szo_y, sz_y, szo_z, sz_z, sy_z,
    ry_y, rzo_y, rz_y, rzo_z, rz_z, ry_z,
    gath, deriv, acc, rd, rq, rx, ryl, tf, sgb, fgb, inv1, inv2,
    v_sem, rs_s, rs_r, ag_s, ag_r, rg_s, rg_r, rr_s, rr_r,
):
    row, col = lax.axis_index("row"), lax.axis_index("col")
    x, yl, core = row // 4, (row // 2) % 2, row % 2
    z, y = col // 2, col % 2
    zp, zm, zo = (z + 1) % 4, (z + 3) % 4, (z + 2) % 4
    xp, xm, xo = (x + 1) % 4, (x + 3) % 4, (x + 2) % 4
    yo, ylo, co = 1 - y, 1 - yl, 1 - core

    def at_row(ax, ayl, ac):
        return (ax * 2 + ayl) * 2 + ac

    dev_z = ((row, zp * 2 + y), (row, zm * 2 + y))
    dev_y = (row, z * 2 + yo)
    dev_row = [(at_row(ax, yl, core), col) for ax in (xp, xm, xo)]
    dev_row += [(at_row(ax, ylo, core), col) for ax in (x, xp, xm, xo)]
    dev_row += [(at_row(x, yl, co), col)]

    barrier = pltpu.get_barrier_semaphore()
    for dev in (*dev_z, dev_y, *dev_row):
        pl.semaphore_signal(barrier, inc=1, device_id=dev, device_id_type=MESH)

    def copy(src, dst, send, recv, dev):
        return pltpu.make_async_remote_copy(
            src_ref=src, dst_ref=dst, send_sem=send, recv_sem=recv, device_id=dev, device_id_type=MESH
        )

    load1 = pltpu.make_async_copy(v1_hbm, v1.at[pl.ds(0, 72)], v_sem.at[0])
    load2 = pltpu.make_async_copy(v2_hbm, v2.at[pl.ds(0, 72)], v_sem.at[1])
    load1.start()
    load2.start()
    for g in range(NG):
        panel[0, g, row // 2, core] = x_in[pl.ds(g * GR, GR)]
        panel[1, g, row // 2, core] = c_in[pl.ds(g * GR, GR)]
    pl.semaphore_wait(barrier, 11)


    order = [(x, yl), (x, ylo), (xp, yl), (xm, yl), (xo, yl), (xp, ylo), (xm, ylo), (xo, ylo)]
    all_x = (xp, xm, xo)
    from_x = (xm, xp, xo)

    def gather_step(p, g, step, direct=False):
        def rg(k, src, ax, ayl):
            return copy(src, src, rg_s.at[p, g, 0], rg_r.at[p, g, k], (at_row(ax, ayl, core), col))

        def piece(ax, ayl):
            return panel.at[p, g, ax * 2 + ayl, core]

        def over_yl(side):
            return rg(0, piece(x, side), x, ylo)

        def own_x(d, at):
            return rg(1 + d, piece(at, yl), all_x[d], yl)

        def other_x(d, at):
            if direct:
                return rg(4 + d, piece(at, ylo if at is not x else yl), all_x[d], ylo)
            return rg(4 + d, piece(at, ylo), all_x[d], yl)

        def core_copy(src):
            return copy(src, src, rg_s.at[p, g, 1], rg_r.at[p, g, 7], (at_row(x, yl, co), col))

        def to_core(i):
            return core_copy(piece(*order[i]))

        if step == 0:
            over_yl(yl).start()
            for d in range(3):
                own_x(d, x).start()
            if direct:
                for d in range(3):
                    other_x(d, x).start()
            to_core(0).start()
        if step == 1:
            over_yl(ylo).wait_recv()
            if not direct:
                for d in range(3):
                    other_x(d, x).start()
            to_core(1).start()
        if step == 2:
            for d in range(3):
                own_x(d, from_x[d]).wait_recv()
                to_core(2 + (1, 0, 2)[d]).start()
        if step == 3:
            for d in range(3):
                other_x(d, from_x[d]).wait_recv()
                to_core(5 + (1, 0, 2)[d]).start()
        if step == 4:
            rg(0, panel.at[p, g, pl.ds(0, 7), core], x, ylo).wait_send()
            core_copy(panel.at[p, g, :, core]).wait_send()
            core_copy(panel.at[p, g, :, co]).wait_recv()

    def slot_table(table, blocks, base, rows, width, slots):
        def fill(i, carry):
            names = [blocks[k, i] - base for k in range(slots)]
            for h in range(width):
                found = jnp.int32(rows * slots)
                for k in range(slots):
                    found = jnp.where(names[k] == h, i * slots + k, found)
                table[i, h] = found
            return carry

        lax.fori_loop(0, rows, fill, 0)

    for step in range(5):
        gather_step(0, 0, step, direct=True)
        if step == 0:
            v1[72] = jnp.zeros((BLK, BLK), jnp.bfloat16)
            v2[72] = jnp.zeros((BLK, BLK), jnp.bfloat16)
            acc[...] = jnp.zeros(acc.shape, jnp.float32)
            slot_table(inv1, blocks1, row * 24, 12, 24, 6)
            slot_table(inv2, blocks2, col * 12, 24, 12, 3)
        if step == 1:
            gather_step(0, 1, 0)
        if step == 3:
            gather_step(0, 1, 1)
            gather_step(0, 2, 0)
    load1.wait()
    load2.wait()

    def dense1(c):
        for i in range(12):
            for h in range(CB):
                wd1[pl.ds(i * BLK, BLK), pl.ds(h * BLK, BLK)] = v1[inv1[i, c * CB + h]]
        return wd1[...]

    def dense2(c):
        for h in range(CB):
            for i in range(12):
                wd2[pl.ds(h * BLK, BLK), pl.ds(i * BLK, BLK)] = v2[inv2[c * CB + h, i]]
        return wd2[...]

    yw, zw = pl.ds(0, YW), pl.ds(YW, ZW)
    yh = (pl.ds(0, YW // 2), pl.ds(YW // 2, YW // 2))
    zh = (pl.ds(YW, ZW // 2), pl.ds(YW + ZW // 2, ZW // 2))
    tgt, src_z = (zp, zm), (zm, zp)

    def rs(u, k, src, dst, dev):
        return copy(src, dst, rs_s.at[u % NT, k], rs_r.at[u % NR, k], dev)

    def rs_y_y(u):
        return rs(u, 0, sy_y.at[u % NT], ry_y.at[u % NS], dev_y)

    def rs_zo_y(u, d):
        return rs(u, 1 + d, szo_y.at[u % NT, d], rzo_y.at[u % NS, d], dev_z[d])

    def rs_z_y(u, d):
        return rs(u, 3 + d, sz_y.at[u % NT, d], rz_y.at[u % NS, d], dev_z[d])

    def rs_zo_z(u, d):
        return rs(u, 5 + d, szo_z.at[u % NT, d], rzo_z.at[u % NS, d], dev_z[d])

    def rs_z_z(u, d):
        return rs(u, 7 + d, sz_z.at[u % NT, d], rz_z.at[u % NS, d], dev_z[d])

    def rs_y_z(u):
        return rs(u, 9, sy_z.at[u % NT], ry_z.at[u % NS], dev_y)

    def product(u):
        sp, s2 = u % NP, u % NT
        g, c = (u // NC) % NG, u % NC

        @pl.when(u < NN)
        def _():
            r = dot(panel[0, g].reshape(16 * GR, DW), dense1(c), 1, 0)
            part[sp] = r.reshape(4, 2, SR, CW)

        @pl.when(u >= NN)
        def _():
            r = dot(panel[1, g].reshape(16 * GR, DW), dense2(c), 1, 1)
            part[sp] = r.reshape(4, 2, SR, CW)

        sy_y[s2] = bf16(part[sp, :, yo, :, yw])
        rs_y_y(u).start()
        for d in range(2):
            szo_z[s2, d] = bf16(part[sp, zo, :, :, zh[d]])
            rs_zo_z(u, d).start()

    def stage2(u):
        s, sp, s2 = u % NS, u % NP, u % NT
        rs_y_y(u).wait()
        for d in range(2):
            szo_y[s2, d] = bf16(part[sp, zo, y, :, yh[d]] + f32(ry_y[s, zo, :, yh[d]]))
            rs_zo_y(u, d).start()
        for d in range(2):
            rs_zo_z(u, d).wait()
            for e in range(2):
                total = part[sp, tgt[d], :, :, zh[e]]
                if e == d:
                    total = total + f32(rzo_z[s, d])
                sz_z[s2, d, :, :, pl.ds(e * (ZW // 2), ZW // 2)] = bf16(total)
            rs_z_z(u, d).start()

    def stage3(u):
        s, sp, s2 = u % NS, u % NP, u % NT
        for d in range(2):
            rs_zo_y(u, d).wait()
            for e in range(2):
                total = part[sp, tgt[d], y, :, yh[e]] + f32(ry_y[s, tgt[d], :, yh[e]])
                if e == d:
                    total = total + f32(rzo_y[s, d])
                sz_y[s2, d, :, yh[e]] = bf16(total)
            rs_z_y(u, d).start()
        for d in range(2):
            rs_z_z(u, d).wait()
        sy_z[s2] = bf16(part[sp, z, yo, :, zw] + f32(rz_z[s, 0, yo]) + f32(rz_z[s, 1, yo]))
        rs_y_z(u).start()

    def stage4(u):
        s, sp = u % NS, u % NP
        g, c = (u // NC) % NG, u % NC
        for d in range(2):
            rs_z_y(u, d).wait()
        sum_y = part[sp, z, y, :, yw] + f32(ry_y[s, z]) + f32(rz_y[s, 0]) + f32(rz_y[s, 1])
        rs_y_z(u).wait()
        sum_z = part[sp, z, y, :, zw] + f32(rz_z[s, 0, y]) + f32(rz_z[s, 1, y]) + f32(ry_z[s])

        def keep(p, first_block, value):
            for b in range(value.shape[1] // BLK):
                gath[p, c * CB + first_block + b, g, z, y] = bf16(value[:, b * BLK : (b + 1) * BLK])

        @pl.when(u < NN)
        def _():
            for lo, cols, total in ((0, yw, sum_y), (YB, zw, sum_z)):
                activated, derivative = gelu_pair(total)
                keep(0, lo, activated)
                deriv[u, :, cols] = derivative

        @pl.when(u >= NN)
        def _():
            for lo, cols, total in ((0, yw, sum_y), (YB, zw, sum_z)):
                keep(1, lo, total * deriv[u - NN, :, cols])

    def ag_of(u, p):
        g, c = (u // NC) % NG, u % NC

        def part_of(first_block, blocks, first_row, rows):
            return lambda at, side: gath.at[
                p, pl.ds(c * CB + first_block, blocks), g, at, side, pl.ds(first_row, rows)
            ]

        if p == 0:
            yb, zb = part_of(0, CB, 0, GR), part_of(0, CB, GR, GR)
            yhalf = [part_of(d * CB // 2, CB // 2, 0, GR) for d in range(2)]
            zhalf = [part_of(d * CB // 2, CB // 2, GR, GR) for d in range(2)]
        else:
            zb_n = CB - AB
            yb, zb = part_of(0, AB, 0, SR), part_of(AB, zb_n, 0, SR)
            yhalf = [part_of(d * AB // 2, AB // 2, 0, SR) for d in range(2)]
            zhalf = [part_of(AB + d * zb_n // 2, zb_n // 2, 0, SR) for d in range(2)]
        every = slice(None)

        def ag(k, ref, dev):
            return copy(ref, ref, ag_s.at[u % NT, k], ag_r.at[u % NR, k], dev)

        return (
            lambda side: ag(0, yb(z, side), dev_y),
            lambda d, at: ag(1 + d, yb(at, every), dev_z[d]),
            lambda d, at: ag(3 + d, yhalf[d](at, every), dev_z[d]),
            lambda d, at: ag(5 + d, zb(at, y), dev_z[d]),
            lambda d, at: ag(7 + d, zhalf[d](at, y), dev_z[d]),
            lambda side: ag(9, zb(every, side), dev_y),
        )

    def either(fn):
        def run(u):
            for p in range(2):
                @pl.when(u // NN == p)
                def _():
                    fn(*ag_of(u, p))

        return run

    @either
    def gather1(y_y, z_y, zo_y, z_z, zo_z, y_z):
        y_y(y).start()
        for d in range(2):
            z_z(d, z).start()

    @either
    def gather2(y_y, z_y, zo_y, z_z, zo_z, y_z):
        y_y(yo).wait_recv()
        for d in range(2):
            z_y(d, z).start()
        for d in range(2):
            z_z(d, src_z[d]).wait_recv()
            zo_z(d, src_z[d]).start()
        y_y(y).wait_send()
        for d in range(2):
            z_z(d, z).wait_send()

    @either
    def gather3(y_y, z_y, zo_y, z_z, zo_z, y_z):
        for d in range(2):
            z_y(d, src_z[d]).wait_recv()
            zo_y(d, src_z[d]).start()
        for d in range(2):
            zo_z(d, zo).wait_recv()
        y_z(y).start()
        for d in range(2):
            z_y(d, z).wait_send()
            zo_z(d, src_z[d]).wait_send()

    @either
    def gather4(y_y, z_y, zo_y, z_z, zo_z, y_z):
        for d in range(2):
            zo_y(d, zo).wait_recv()
        y_z(yo).wait_recv()
        y_z(y).wait_send()
        for d in range(2):
            zo_y(d, src_z[d]).wait_send()

    def use(u):
        p, g, c = u // NN, (u // NC) % NG, u % NC
        rows = jnp.concatenate([gath[p, c * CB + b, g].reshape(16 * GR, BLK) for b in range(CB)], axis=1)

        @pl.when(p == 0)
        def _():
            acc[0, g] += dot(rows, dense2(c), 1, 0).reshape(8, 2, GR, DW)

        @pl.when(p == 1)
        def _():
            acc[1, g] += dot(rows, dense1(c), 1, 1).reshape(8, 2, GR, DW)

    def local_block(blocks, i, k, base, width):
        return jnp.clip(blocks[k, i] - base, 0, width - 1)

    def second_out(j):
        return pltpu.make_async_copy(sgb.at[j % 2], sg_ref.at[j], v_sem.at[2 + j % 2])

    def second(j):
        flipped = gath[0, j].reshape(16 * OWN, BLK).T
        picked = jnp.concatenate([cblk[local_block(blocks2, j, k, col * 12, 12)] for k in range(3)], axis=1)
        g = bf16(dot(flipped, picked, 1, 0))

        @pl.when(j >= 2)
        def _():
            second_out(j - 2).wait()

        for k in range(3):
            sgb[j % 2, k] = g[:, k * BLK : (k + 1) * BLK]
        second_out(j).start()

    def first_out(i):
        return pltpu.make_async_copy(fgb.at[i % 2], fg_ref.at[i], v_sem.at[4 + i % 2])

    def first(i):
        picked = jnp.concatenate([gath[1, local_block(blocks1, i, k, row * 24, 24)].reshape(16 * OWN, BLK) for k in range(6)], axis=1)
        g = bf16(dot(xt[pl.ds(i * BLK, BLK), :], picked, 1, 0))
        if i >= 2:
            first_out(i - 2).wait()
        for k in range(6):
            fgb[i % 2, k] = g[:, k * BLK : (k + 1) * BLK]
        first_out(i).start()

    def scatter_step(p, g, step, direct=False):
        e = p * NG + g

        def rr(k, src, dst, ax, ayl, ac=core):
            send = rr_s.at[e, 0 if k == 0 else 2 if k == 7 else 1]
            return copy(src, dst, send, rr_r.at[e, k], (at_row(ax, ayl, ac), col))

        def over_core():
            return rr(0, acc.at[p, g, :, co], rd.at[g], x, yl, co)

        def over_x(d, b=None):
            if b is None:
                return rr(1 + d, rq.at[g, all_x[d]], rx.at[g, d], all_x[d], yl)
            return rr(1 + 2 * d + b, rq.at[g, all_x[d], (yl, ylo)[b]], rx.at[g, d, b], all_x[d], (yl, ylo)[b])

        def over_yl():
            return rr(7, tf.at[g], ryl.at[g], x, ylo)

        def sent():
            rr(1, rq.at[g, pl.ds(0, 3)], rx.at[g], xp, yl).wait_send()

        def own_sum(ax, ayl):
            return acc[p, g, ax * 2 + ayl, core] + rd[g, ax * 2 + ayl]

        if step == 0:
            over_core().start()
        if step == 1:
            over_core().wait()
            if direct:
                tf[g] = bf16(own_sum(x, ylo))
                over_yl().start()
            for d in (2, 0, 1):
                for b in range(2):
                    rq[g, all_x[d], b] = bf16(own_sum(all_x[d], b))
                if direct:
                    for b in range(2):
                        over_x(d, b).start()
                else:
                    over_x(d).start()
        if step == 2 and not direct:
            for d in range(3):
                over_x(d).wait_recv()
            sent()
            tf[g] = bf16(own_sum(x, ylo) + f32(rx[g, 0, ylo]) + f32(rx[g, 1, ylo]) + f32(rx[g, 2, ylo]))
            over_yl().start()
        if step == 3:
            total = own_sum(x, yl)
            for d in range(3):
                if direct:
                    for b in range(2):
                        over_x(d, b).wait_recv()
                        total = total + f32(rx[g, d, b])
                else:
                    total = total + f32(rx[g, d, yl])
            if direct:
                sent()
            over_yl().wait()
            total = bf16(total + f32(ryl[g]))
            rows = pl.ds(pl.multiple_of(g * GR, GR), GR)

            @pl.when(p == 0)
            def _():
                out_ref[rows, :] = total

            @pl.when(p == 1)
            def _():
                ig_ref[rows, :] = total

    def rs_unit(t):
        late = t - NN
        u = jnp.where(t < NN, t, NN + late // 2)
        return u, (t >= 0) & (t < 3 * NN) & ((t < NN) | (late % 2 == 0))

    def ag_unit(t):
        early = t - AG1
        u = jnp.where(t < AG2, early // 2, NN + t - AG2)
        return u, ((t >= AG1) & (t < AG2) & (early % 2 == 0)) | ((t >= AG2) & (t < AG2 + NN))

    def at_ticks(steps):
        def find(t):
            n, ok = jnp.int32(0), jnp.bool_(False)
            for e, at in steps:
                n = n + jnp.where(t == at, e, 0)
                ok = ok | (t == at)
            return n, ok

        return find

    gathers = [
        (1, (None, None, 0, 2, 3)),
        (2, (None, 2, 4, 6, 7)),
        (3, (1, 4, 7, 9, 11)),
        (4, (7, 10, 13, 16, 19)),
        (5, (13, 16, 19, 22, 25)),
    ]
    scatters = [(g, AG1 + 2 * (NC * g + NC - 1) + A4 + 1) for g in range(NG)]
    scatters += [(NG + g, AG2 + NC * g + NC - 1 + A4 + 1) for g in range(NG - 1)]
    scatters = [(e, tuple(start + 2 * k for k in range(4))) for e, start in scatters]

    def tick(t, carry):
        def run(offset, unit_of, fn):
            u, ok = unit_of(t - offset)

            @pl.when(ok)
            def _():
                fn(u)

        run(A4, ag_unit, gather4)
        run(A3, ag_unit, gather3)
        run(A2, ag_unit, gather2)
        run(S4, rs_unit, stage4)
        run(0, ag_unit, gather1)
        run(S3, rs_unit, stage3)
        run(S2, rs_unit, stage2)
        run(0, rs_unit, product)
        for step in range(4, -1, -1):
            run(0, at_ticks([(e, ticks[step]) for e, ticks in gathers if ticks[step] is not None]),
                lambda e, step=step: gather_step(e // NG, e % NG, step))
        for step in range(3, -1, -1):
            run(0, at_ticks([(e, ticks[step]) for e, ticks in scatters if ticks[step] < TICKS]),
                lambda e, step=step: scatter_step(e // NG, e % NG, step))
        run(A4, ag_unit, use)

        @pl.when(t == 28)
        def _():
            for c in range(12):
                cblk[c] = panel[1, :, :, :, :, c * BLK : (c + 1) * BLK].reshape(16 * OWN, BLK)

        @pl.when(t == 30)
        def _():
            xt[...] = panel[0].reshape(16 * OWN, DW).T

        @pl.when((t >= SG) & (t < SG + 12))
        def _():
            second(2 * (t - SG))
            second(2 * (t - SG) + 1)

        return carry

    lax.fori_loop(0, TICKS, tick, 0)
    scatter_step(1, NG - 1, 0, direct=True)
    scatter_step(1, NG - 2, 2)
    scatter_step(1, NG - 1, 1, direct=True)
    first(0)
    scatter_step(1, NG - 2, 3)
    for i in range(1, 12):
        first(i)
    scatter_step(1, NG - 1, 3, direct=True)
    for i in range(2):
        second_out(22 + i).wait()
        first_out(10 + i).wait()


def hand_over(*refs):
    ins, outs, bufs, (sem_in, sem_out) = refs[:4], refs[4:8], refs[8:12], refs[12:]
    loads, stores = [], []
    for src, dst, buf in zip(ins, outs, bufs):
        pieces = 6 if len(src.shape) == 4 else 1
        size = src.shape[0] // pieces
        for k in range(pieces):
            rows = pl.ds(k * size, size)
            n = len(loads)
            loads.append(pltpu.make_async_copy(src.at[rows], buf.at[rows], sem_in.at[n]))
            stores.append(pltpu.make_async_copy(buf.at[rows], dst.at[rows], sem_out.at[n]))
    for load in loads:
        load.start()
    for load, store in zip(loads, stores):
        load.wait()
        store.start()
    for store in stores:
        store.wait()


def shards(inputs, first_values, first_blocks, second_values, second_blocks, cotangent):
    bf, fl = jnp.bfloat16, jnp.float32
    smem = pl.BlockSpec(memory_space=pltpu.SMEM)
    vmem = pl.BlockSpec(memory_space=pltpu.VMEM)
    dma = pltpu.SemaphoreType.DMA
    v1 = first_values.reshape(72, BLK, BLK)
    v2 = second_values.reshape(72, BLK, BLK)
    results = pl.pallas_call(
        kernel,
        out_shape=(
            jax.ShapeDtypeStruct((OWN, DW), bf),
            jax.ShapeDtypeStruct((OWN, DW), bf),
            jax.ShapeDtypeStruct((12, 6, BLK, BLK), bf),
            jax.ShapeDtypeStruct((24, 3, BLK, BLK), bf),
        ),
        in_specs=[smem] * 2 + [vmem] * 2 + [pl.BlockSpec(memory_space=pl.ANY)] * 2,
        out_specs=(vmem,) * 2 + (pl.BlockSpec(memory_space=pl.ANY),) * 2,
        scratch_shapes=[
            pltpu.VMEM((2, NG, 8, 2, GR, DW), bf),
            pltpu.VMEM((12, 16 * OWN, BLK), bf),
            pltpu.VMEM((DW, 16 * OWN), bf),
            pltpu.VMEM((73, BLK, BLK), bf),
            pltpu.VMEM((73, BLK, BLK), bf),
            pltpu.VMEM((DW, CW), bf),
            pltpu.VMEM((CW, DW), bf),
            pltpu.VMEM((NP, 4, 2, SR, CW), fl),
            pltpu.VMEM((NT, 4, SR, YW), bf),
            pltpu.VMEM((NT, 2, SR, YW // 2), bf),
            pltpu.VMEM((NT, 2, SR, YW), bf),
            pltpu.VMEM((NT, 2, 2, SR, ZW // 2), bf),
            pltpu.VMEM((NT, 2, 2, SR, ZW), bf),
            pltpu.VMEM((NT, SR, ZW), bf),
            pltpu.VMEM((NS, 4, SR, YW), bf),
            pltpu.VMEM((NS, 2, SR, YW // 2), bf),
            pltpu.VMEM((NS, 2, SR, YW), bf),
            pltpu.VMEM((NS, 2, 2, SR, ZW // 2), bf),
            pltpu.VMEM((NS, 2, 2, SR, ZW), bf),
            pltpu.VMEM((NS, SR, ZW), bf),
            pltpu.VMEM((2, NC * CB, NG, 4, 2, SR, BLK), bf),
            pltpu.VMEM((NN, SR, CW), fl),
            pltpu.VMEM((2, NG, 8, 2, GR, DW), fl),
            pltpu.VMEM((NG, 8, GR, DW), fl),
            pltpu.VMEM((NG, 4, 2, GR, DW), bf),
            pltpu.VMEM((NG, 3, 2, GR, DW), bf),
            pltpu.VMEM((NG, GR, DW), bf),
            pltpu.VMEM((NG, GR, DW), bf),
            pltpu.VMEM((2, 3, BLK, BLK), bf),
            pltpu.VMEM((2, 6, BLK, BLK), bf),
            pltpu.SMEM((12, 24), jnp.int32),
            pltpu.SMEM((24, 12), jnp.int32),
            dma((6,)),
            dma((NT, 10)), dma((NR, 10)), dma((NT, 10)), dma((NR, 10)),
            dma((2, NG, 2)), dma((2, NG, 8)), dma((2 * NG, 3)), dma((2 * NG, 8)),
        ],
        compiler_params=pltpu.CompilerParams(
            collective_id=1, has_side_effects=True, vmem_limit_bytes=62 * 2**20
        ),
        name="sparse_ffn",
    )(first_blocks.T, second_blocks.T, inputs, cotangent, v1, v2)
    anywhere = pl.BlockSpec(memory_space=pl.ANY)
    return pl.pallas_call(
        hand_over,
        out_shape=tuple(jax.ShapeDtypeStruct(r.shape, r.dtype) for r in results),
        in_specs=[anywhere] * 4,
        out_specs=(anywhere,) * 4,
        scratch_shapes=[pltpu.VMEM(r.shape, r.dtype) for r in results] + [dma((14,)), dma((14,))],
        name="hand_over",
    )(*results)


def solution(mesh):
    placed = (
        P("row", "col"),
        P("col", "row", None, None),
        P("col", "row"),
        P("row", "col", None, None),
        P("row", "col"),
        P("row", "col"),
    )
    return jax.shard_map(
        shards,
        mesh=mesh,
        in_specs=placed,
        out_specs=(
            P("row", "col"),
            P("row", "col"),
            P("col", "row", None, None),
            P("row", "col", None, None),
        ),
        check_vma=False,
    )
```

```python
import jax
import jax.numpy as jnp
from jax import lax
from jax.experimental import pallas as pl
from jax.experimental.pallas import tpu as pltpu
from jax.sharding import PartitionSpec as P

MESH = pl.DeviceIdType.MESH
gelu_scale = 0.7978845608028654
gelu_cubic = 0.044715

BLK = 128
NG = 3
NC = 4
CB = 6
CW = CB * BLK
YB = 2
AB = 4
YW, ZW = YB * BLK, (CB - YB) * BLK
NN = NG * NC
NU = 2 * NN
NS = 12
NR = 7
NT = 3
NP = 9
GR = 16
SR = 2 * GR
OWN = NG * GR
DW = 1536
S2, S3, S4 = 3, 6, 9
A2, A3, A4 = 3, 6, 9
AG1, AG2 = NN + 1, 3 * NN
TICKS = AG2 + NN + A4
SG = AG1 + 2 * NN + A4 - 1


def gelu_pair(pre_act):
    inner_arg = gelu_scale * (pre_act + gelu_cubic * pre_act * pre_act * pre_act)
    tanh_value = jnp.tanh(inner_arg)
    activated = 0.5 * pre_act * (1.0 + tanh_value)
    derivative = 0.5 * (1.0 + tanh_value) + 0.5 * pre_act * (
        1.0 - tanh_value * tanh_value
    ) * gelu_scale * (1.0 + 3.0 * gelu_cubic * pre_act * pre_act)
    return (activated, derivative)


def f32(v):
    return v.astype(jnp.float32)


def bf16(v):
    return v.astype(jnp.bfloat16)


def dot(a, b, ca, cb):
    return lax.dot_general(a, b, (((ca,), (cb,)), ((), ())), preferred_element_type=jnp.float32)


def kernel(
    blocks1, blocks2, x_in, c_in, v1_hbm, v2_hbm,
    out_ref, ig_ref, fg_ref, sg_ref,
    panel, cblk, xt, v1, v2, wd1, wd2, part, sy_y, szo_y, sz_y, szo_z, sz_z, sy_z,
    ry_y, rzo_y, rz_y, rzo_z, rz_z, ry_z,
    gath, deriv, acc, rd, rq, rx, ryl, tf, sgb, fgb, inv1, inv2,
    v_sem, rs_s, rs_r, ag_s, ag_r, rg_s, rg_r, rr_s, rr_r,
):
    row, col = lax.axis_index("row"), lax.axis_index("col")
    x, yl, core = row // 4, (row // 2) % 2, row % 2
    z, y = col // 2, col % 2
    zp, zm, zo = (z + 1) % 4, (z + 3) % 4, (z + 2) % 4
    xp, xm, xo = (x + 1) % 4, (x + 3) % 4, (x + 2) % 4
    yo, ylo, co = 1 - y, 1 - yl, 1 - core

    def at_row(ax, ayl, ac):
        return (ax * 2 + ayl) * 2 + ac

    dev_z = ((row, zp * 2 + y), (row, zm * 2 + y))
    dev_y = (row, z * 2 + yo)
    dev_row = [(at_row(ax, yl, core), col) for ax in (xp, xm, xo)]
    dev_row += [(at_row(ax, ylo, core), col) for ax in (x, xp, xm, xo)]
    dev_row += [(at_row(x, yl, co), col)]

    barrier = pltpu.get_barrier_semaphore()
    for dev in (*dev_z, dev_y, *dev_row):
        pl.semaphore_signal(barrier, inc=1, device_id=dev, device_id_type=MESH)

    def copy(src, dst, send, recv, dev):
        return pltpu.make_async_remote_copy(
            src_ref=src, dst_ref=dst, send_sem=send, recv_sem=recv, device_id=dev, device_id_type=MESH
        )

    load1 = pltpu.make_async_copy(v1_hbm, v1.at[pl.ds(0, 72)], v_sem.at[0])
    load2 = pltpu.make_async_copy(v2_hbm, v2.at[pl.ds(0, 72)], v_sem.at[1])
    load1.start()
    load2.start()
    for g in range(NG):
        panel[0, g, row // 2, core] = x_in[pl.ds(g * GR, GR)]
        panel[1, g, row // 2, core] = c_in[pl.ds(g * GR, GR)]
    pl.semaphore_wait(barrier, 11)


    order = [(x, yl), (x, ylo), (xp, yl), (xm, yl), (xo, yl), (xp, ylo), (xm, ylo), (xo, ylo)]
    all_x = (xp, xm, xo)
    from_x = (xm, xp, xo)

    def gather_step(p, g, step, direct=False):
        def rg(k, src, ax, ayl):
            return copy(src, src, rg_s.at[p, g, 0], rg_r.at[p, g, k], (at_row(ax, ayl, core), col))

        def piece(ax, ayl):
            return panel.at[p, g, ax * 2 + ayl, core]

        def over_yl(side):
            return rg(0, piece(x, side), x, ylo)

        def own_x(d, at):
            return rg(1 + d, piece(at, yl), all_x[d], yl)

        def other_x(d, at):
            if direct:
                return rg(4 + d, piece(at, ylo if at is not x else yl), all_x[d], ylo)
            return rg(4 + d, piece(at, ylo), all_x[d], yl)

        def core_copy(src):
            return copy(src, src, rg_s.at[p, g, 1], rg_r.at[p, g, 7], (at_row(x, yl, co), col))

        def to_core(i):
            return core_copy(piece(*order[i]))

        if step == 0:
            over_yl(yl).start()
            for d in range(3):
                own_x(d, x).start()
            if direct:
                for d in range(3):
                    other_x(d, x).start()
            to_core(0).start()
        if step == 1:
            over_yl(ylo).wait_recv()
            if not direct:
                for d in range(3):
                    other_x(d, x).start()
            to_core(1).start()
        if step == 2:
            for d in range(3):
                own_x(d, from_x[d]).wait_recv()
                to_core(2 + (1, 0, 2)[d]).start()
        if step == 3:
            for d in range(3):
                other_x(d, from_x[d]).wait_recv()
                to_core(5 + (1, 0, 2)[d]).start()
        if step == 4:
            rg(0, panel.at[p, g, pl.ds(0, 7), core], x, ylo).wait_send()
            core_copy(panel.at[p, g, :, core]).wait_send()
            core_copy(panel.at[p, g, :, co]).wait_recv()

    def slot_table(table, blocks, base, rows, width, slots):
        def fill(i, carry):
            names = [blocks[k, i] - base for k in range(slots)]
            for h in range(width):
                found = jnp.int32(rows * slots)
                for k in range(slots):
                    found = jnp.where(names[k] == h, i * slots + k, found)
                table[i, h] = found
            return carry

        lax.fori_loop(0, rows, fill, 0)

    for step in range(5):
        gather_step(0, 0, step, direct=True)
        if step == 0:
            v1[72] = jnp.zeros((BLK, BLK), jnp.bfloat16)
            v2[72] = jnp.zeros((BLK, BLK), jnp.bfloat16)
            acc[...] = jnp.zeros(acc.shape, jnp.float32)
            slot_table(inv1, blocks1, row * 24, 12, 24, 6)
            slot_table(inv2, blocks2, col * 12, 24, 12, 3)
        if step == 1:
            gather_step(0, 1, 0)
        if step == 3:
            gather_step(0, 1, 1)
            gather_step(0, 2, 0)
    load1.wait()
    load2.wait()

    def dense1(c):
        for i in range(12):
            for h in range(CB):
                wd1[pl.ds(i * BLK, BLK), pl.ds(h * BLK, BLK)] = v1[inv1[i, c * CB + h]]
        return wd1[...]

    def dense2(c):
        for h in range(CB):
            for i in range(12):
                wd2[pl.ds(h * BLK, BLK), pl.ds(i * BLK, BLK)] = v2[inv2[c * CB + h, i]]
        return wd2[...]

    yw, zw = pl.ds(0, YW), pl.ds(YW, ZW)
    yh = (pl.ds(0, YW // 2), pl.ds(YW // 2, YW // 2))
    zh = (pl.ds(YW, ZW // 2), pl.ds(YW + ZW // 2, ZW // 2))
    tgt, src_z = (zp, zm), (zm, zp)

    def rs(u, k, src, dst, dev):
        return copy(src, dst, rs_s.at[u % NT, k], rs_r.at[u % NR, k], dev)

    def rs_y_y(u):
        return rs(u, 0, sy_y.at[u % NT], ry_y.at[u % NS], dev_y)

    def rs_zo_y(u, d):
        return rs(u, 1, szo_y.at[u % NT, d], rzo_y.at[u % NS, d], dev_z[d])

    def rs_z_y(u, d):
        return rs(u, 2, sz_y.at[u % NT, d], rz_y.at[u % NS, d], dev_z[d])

    def rs_zo_z(u, d):
        return rs(u, 3, szo_z.at[u % NT, d], rzo_z.at[u % NS, d], dev_z[d])

    def rs_z_z(u, d):
        return rs(u, 4, sz_z.at[u % NT, d], rz_z.at[u % NS, d], dev_z[d])

    def rs_y_z(u):
        return rs(u, 5, sy_z.at[u % NT], ry_z.at[u % NS], dev_y)

    def rs_both(u, k, sent, got):
        rs(u, k, sent.at[u % NT], got.at[u % NS], dev_z[0]).wait()

    def product(u):
        sp, s2 = u % NP, u % NT
        g, c = (u // NC) % NG, u % NC

        @pl.when(u < NN)
        def _():
            r = dot(panel[0, g].reshape(16 * GR, DW), dense1(c), 1, 0)
            part[sp] = r.reshape(4, 2, SR, CW)

        @pl.when(u >= NN)
        def _():
            r = dot(panel[1, g].reshape(16 * GR, DW), dense2(c), 1, 1)
            part[sp] = r.reshape(4, 2, SR, CW)

        sy_y[s2] = bf16(part[sp, :, yo, :, yw])
        rs_y_y(u).start()
        for d in range(2):
            szo_z[s2, d] = bf16(part[sp, zo, :, :, zh[d]])
            rs_zo_z(u, d).start()

    def stage2(u):
        s, sp, s2 = u % NS, u % NP, u % NT
        rs_y_y(u).wait()
        for d in range(2):
            szo_y[s2, d] = bf16(part[sp, zo, y, :, yh[d]] + f32(ry_y[s, zo, :, yh[d]]))
            rs_zo_y(u, d).start()
        rs_both(u, 3, szo_z, rzo_z)
        for d in range(2):
            for e in range(2):
                total = part[sp, tgt[d], :, :, zh[e]]
                if e == d:
                    total = total + f32(rzo_z[s, d])
                sz_z[s2, d, :, :, pl.ds(e * (ZW // 2), ZW // 2)] = bf16(total)
            rs_z_z(u, d).start()

    def stage3(u):
        s, sp, s2 = u % NS, u % NP, u % NT
        rs_both(u, 1, szo_y, rzo_y)
        for d in range(2):
            for e in range(2):
                total = part[sp, tgt[d], y, :, yh[e]] + f32(ry_y[s, tgt[d], :, yh[e]])
                if e == d:
                    total = total + f32(rzo_y[s, d])
                sz_y[s2, d, :, yh[e]] = bf16(total)
            rs_z_y(u, d).start()
        rs_both(u, 4, sz_z, rz_z)
        sy_z[s2] = bf16(part[sp, z, yo, :, zw] + f32(rz_z[s, 0, yo]) + f32(rz_z[s, 1, yo]))
        rs_y_z(u).start()

    def stage4(u):
        s, sp = u % NS, u % NP
        g, c = (u // NC) % NG, u % NC
        rs_both(u, 2, sz_y, rz_y)
        sum_y = part[sp, z, y, :, yw] + f32(ry_y[s, z]) + f32(rz_y[s, 0]) + f32(rz_y[s, 1])
        rs_y_z(u).wait()
        sum_z = part[sp, z, y, :, zw] + f32(rz_z[s, 0, y]) + f32(rz_z[s, 1, y]) + f32(ry_z[s])

        def keep(p, first_block, value):
            for b in range(value.shape[1] // BLK):
                gath[p, c * CB + first_block + b, g, z, y] = bf16(value[:, b * BLK : (b + 1) * BLK])

        @pl.when(u < NN)
        def _():
            for lo, cols, total in ((0, yw, sum_y), (YB, zw, sum_z)):
                activated, derivative = gelu_pair(total)
                keep(0, lo, activated)
                deriv[u, :, cols] = derivative

        @pl.when(u >= NN)
        def _():
            for lo, cols, total in ((0, yw, sum_y), (YB, zw, sum_z)):
                keep(1, lo, total * deriv[u - NN, :, cols])

    def ag_of(u, p):
        g, c = (u // NC) % NG, u % NC

        def part_of(first_block, blocks, first_row, rows):
            return lambda at, side: gath.at[
                p, pl.ds(c * CB + first_block, blocks), g, at, side, pl.ds(first_row, rows)
            ]

        if p == 0:
            yb, zb = part_of(0, CB, 0, GR), part_of(0, CB, GR, GR)
            yhalf = [part_of(d * CB // 2, CB // 2, 0, GR) for d in range(2)]
            zhalf = [part_of(d * CB // 2, CB // 2, GR, GR) for d in range(2)]
        else:
            zb_n = CB - AB
            yb, zb = part_of(0, AB, 0, SR), part_of(AB, zb_n, 0, SR)
            yhalf = [part_of(d * AB // 2, AB // 2, 0, SR) for d in range(2)]
            zhalf = [part_of(AB + d * zb_n // 2, zb_n // 2, 0, SR) for d in range(2)]
        every = slice(None)

        def ag(k, ref, dev):
            return copy(ref, ref, ag_s.at[u % NT, k], ag_r.at[u % NR, k], dev)

        return (
            lambda side: ag(0, yb(z, side), dev_y),
            lambda d, at: ag(1 + d, yb(at, every), dev_z[d]),
            lambda d, at: ag(3 + d, yhalf[d](at, every), dev_z[d]),
            lambda d, at: ag(5 + d, zb(at, y), dev_z[d]),
            lambda d, at: ag(7 + d, zhalf[d](at, y), dev_z[d]),
            lambda side: ag(9, zb(every, side), dev_y),
        )

    def either(fn):
        def run(u):
            for p in range(2):
                @pl.when(u // NN == p)
                def _():
                    fn(*ag_of(u, p))

        return run

    @either
    def gather1(y_y, z_y, zo_y, z_z, zo_z, y_z):
        y_y(y).start()
        for d in range(2):
            z_z(d, z).start()

    @either
    def gather2(y_y, z_y, zo_y, z_z, zo_z, y_z):
        y_y(yo).wait_recv()
        for d in range(2):
            z_y(d, z).start()
        for d in range(2):
            z_z(d, src_z[d]).wait_recv()
            zo_z(d, src_z[d]).start()
        y_y(y).wait_send()
        for d in range(2):
            z_z(d, z).wait_send()

    @either
    def gather3(y_y, z_y, zo_y, z_z, zo_z, y_z):
        for d in range(2):
            z_y(d, src_z[d]).wait_recv()
            zo_y(d, src_z[d]).start()
        for d in range(2):
            zo_z(d, zo).wait_recv()
        y_z(y).start()
        for d in range(2):
            z_y(d, z).wait_send()
            zo_z(d, src_z[d]).wait_send()

    @either
    def gather4(y_y, z_y, zo_y, z_z, zo_z, y_z):
        for d in range(2):
            zo_y(d, zo).wait_recv()
        y_z(yo).wait_recv()
        y_z(y).wait_send()
        for d in range(2):
            zo_y(d, src_z[d]).wait_send()

    def use(u):
        p, g, c = u // NN, (u // NC) % NG, u % NC
        rows = jnp.concatenate([gath[p, c * CB + b, g].reshape(16 * GR, BLK) for b in range(CB)], axis=1)

        @pl.when(p == 0)
        def _():
            acc[0, g] += dot(rows, dense2(c), 1, 0).reshape(8, 2, GR, DW)

        @pl.when(p == 1)
        def _():
            acc[1, g] += dot(rows, dense1(c), 1, 1).reshape(8, 2, GR, DW)

    def local_block(blocks, i, k, base, width):
        return jnp.clip(blocks[k, i] - base, 0, width - 1)

    def second_out(j):
        return pltpu.make_async_copy(sgb.at[j % 2], sg_ref.at[j], v_sem.at[2 + j % 2])

    def second(j):
        flipped = gath[0, j].reshape(16 * OWN, BLK).T
        picked = jnp.concatenate([cblk[local_block(blocks2, j, k, col * 12, 12)] for k in range(3)], axis=1)
        g = bf16(dot(flipped, picked, 1, 0))

        @pl.when(j >= 2)
        def _():
            second_out(j - 2).wait()

        for k in range(3):
            sgb[j % 2, k] = g[:, k * BLK : (k + 1) * BLK]
        second_out(j).start()

    def first_out(i):
        return pltpu.make_async_copy(fgb.at[i % 2], fg_ref.at[i], v_sem.at[4 + i % 2])

    def first(i):
        picked = jnp.concatenate([gath[1, local_block(blocks1, i, k, row * 24, 24)].reshape(16 * OWN, BLK) for k in range(6)], axis=1)
        g = bf16(dot(xt[pl.ds(i * BLK, BLK), :], picked, 1, 0))
        if i >= 2:
            first_out(i - 2).wait()
        for k in range(6):
            fgb[i % 2, k] = g[:, k * BLK : (k + 1) * BLK]
        first_out(i).start()

    def scatter_step(p, g, step, direct=False):
        def rr(k, src, dst, ax, ayl, ac=core):
            send = rr_s.at[g, 0 if k == 0 else 2 if k == 7 else 1]
            return copy(src, dst, send, rr_r.at[g, k], (at_row(ax, ayl, ac), col))

        def over_core():
            return rr(0, acc.at[p, g, :, co], rd.at[g], x, yl, co)

        def over_x(d, b=None):
            if b is None:
                return rr(1 + d, rq.at[g, all_x[d]], rx.at[g, d], all_x[d], yl)
            return rr(1 + 2 * d + b, rq.at[g, all_x[d], (yl, ylo)[b]], rx.at[g, d, b], all_x[d], (yl, ylo)[b])

        def over_yl():
            return rr(7, tf.at[g], ryl.at[g], x, ylo)

        def sent():
            rr(1, rq.at[g, pl.ds(0, 3)], rx.at[g], xp, yl).wait_send()

        def own_sum(ax, ayl):
            return acc[p, g, ax * 2 + ayl, core] + rd[g, ax * 2 + ayl]

        if step == 0:
            over_core().start()
        if step == 1:
            over_core().wait()
            if direct:
                tf[g] = bf16(own_sum(x, ylo))
                over_yl().start()
            for d in (2, 0, 1):
                for b in range(2):
                    rq[g, all_x[d], b] = bf16(own_sum(all_x[d], b))
                if direct:
                    for b in range(2):
                        over_x(d, b).start()
                else:
                    over_x(d).start()
        if step == 2 and not direct:
            for d in range(3):
                over_x(d).wait_recv()
            sent()
            tf[g] = bf16(own_sum(x, ylo) + f32(rx[g, 0, ylo]) + f32(rx[g, 1, ylo]) + f32(rx[g, 2, ylo]))
            over_yl().start()
        if step == 3:
            total = own_sum(x, yl)
            for d in range(3):
                if direct:
                    for b in range(2):
                        over_x(d, b).wait_recv()
                        total = total + f32(rx[g, d, b])
                else:
                    total = total + f32(rx[g, d, yl])
            if direct:
                sent()
            over_yl().wait()
            total = bf16(total + f32(ryl[g]))
            rows = pl.ds(pl.multiple_of(g * GR, GR), GR)

            @pl.when(p == 0)
            def _():
                out_ref[rows, :] = total

            @pl.when(p == 1)
            def _():
                ig_ref[rows, :] = total

    def rs_unit(t):
        late = t - NN
        u = jnp.where(t < NN, t, NN + late // 2)
        return u, (t >= 0) & (t < 3 * NN) & ((t < NN) | (late % 2 == 0))

    def ag_unit(t):
        early = t - AG1
        u = jnp.where(t < AG2, early // 2, NN + t - AG2)
        return u, ((t >= AG1) & (t < AG2) & (early % 2 == 0)) | ((t >= AG2) & (t < AG2 + NN))

    def at_ticks(steps):
        def find(t):
            n, ok = jnp.int32(0), jnp.bool_(False)
            for e, at in steps:
                n = n + jnp.where(t == at, e, 0)
                ok = ok | (t == at)
            return n, ok

        return find

    gathers = [
        (1, (None, None, 0, 2, 3)),
        (2, (None, 2, 4, 6, 7)),
        (3, (1, 4, 7, 9, 11)),
        (4, (7, 10, 13, 16, 19)),
        (5, (13, 16, 19, 22, 25)),
    ]
    scatters = [(g, AG1 + 2 * (NC * g + NC - 1) + A4 + 1) for g in range(NG)]
    scatters += [(NG + g, AG2 + NC * g + NC - 1 + A4 + 1) for g in range(NG - 1)]
    scatters = [(e, tuple(start + 2 * k for k in range(4))) for e, start in scatters]

    def tick(t, carry):
        def run(offset, unit_of, fn):
            u, ok = unit_of(t - offset)

            @pl.when(ok)
            def _():
                fn(u)

        run(A4, ag_unit, gather4)
        run(A3, ag_unit, gather3)
        run(A2, ag_unit, gather2)
        run(S4, rs_unit, stage4)
        run(0, ag_unit, gather1)
        run(S3, rs_unit, stage3)
        run(S2, rs_unit, stage2)
        run(0, rs_unit, product)
        for step in range(4, -1, -1):
            run(0, at_ticks([(e, ticks[step]) for e, ticks in gathers if ticks[step] is not None]),
                lambda e, step=step: gather_step(e // NG, e % NG, step))
        for step in range(3, -1, -1):
            run(0, at_ticks([(e, ticks[step]) for e, ticks in scatters if ticks[step] < TICKS]),
                lambda e, step=step: scatter_step(e // NG, e % NG, step))
        run(A4, ag_unit, use)

        @pl.when(t == 28)
        def _():
            for c in range(12):
                cblk[c] = panel[1, :, :, :, :, c * BLK : (c + 1) * BLK].reshape(16 * OWN, BLK)

        @pl.when(t == 30)
        def _():
            xt[...] = panel[0].reshape(16 * OWN, DW).T

        @pl.when((t >= SG) & (t < SG + 12))
        def _():
            second(2 * (t - SG))
            second(2 * (t - SG) + 1)

        return carry

    lax.fori_loop(0, TICKS, tick, 0)
    scatter_step(1, NG - 1, 0, direct=True)
    scatter_step(1, NG - 2, 2)
    scatter_step(1, NG - 1, 1, direct=True)
    first(0)
    scatter_step(1, NG - 2, 3)
    for i in range(1, 12):
        first(i)
    scatter_step(1, NG - 1, 3, direct=True)
    for i in range(2):
        second_out(22 + i).wait()
        first_out(10 + i).wait()


def hand_over(*refs):
    ins, outs, bufs, (sem_in, sem_out) = refs[:4], refs[4:8], refs[8:12], refs[12:]
    loads, stores = [], []
    for src, dst, buf in zip(ins, outs, bufs):
        pieces = 6 if len(src.shape) == 4 else 1
        size = src.shape[0] // pieces
        for k in range(pieces):
            rows = pl.ds(k * size, size)
            n = len(loads)
            loads.append(pltpu.make_async_copy(src.at[rows], buf.at[rows], sem_in.at[n]))
            stores.append(pltpu.make_async_copy(buf.at[rows], dst.at[rows], sem_out.at[n]))
    for load in loads:
        load.start()
    for load, store in zip(loads, stores):
        load.wait()
        store.start()
    for store in stores:
        store.wait()


def shards(inputs, first_values, first_blocks, second_values, second_blocks, cotangent):
    bf, fl = jnp.bfloat16, jnp.float32
    smem = pl.BlockSpec(memory_space=pltpu.SMEM)
    vmem = pl.BlockSpec(memory_space=pltpu.VMEM)
    dma = pltpu.SemaphoreType.DMA
    v1 = first_values.reshape(72, BLK, BLK)
    v2 = second_values.reshape(72, BLK, BLK)
    results = pl.pallas_call(
        kernel,
        out_shape=(
            jax.ShapeDtypeStruct((OWN, DW), bf),
            jax.ShapeDtypeStruct((OWN, DW), bf),
            jax.ShapeDtypeStruct((12, 6, BLK, BLK), bf),
            jax.ShapeDtypeStruct((24, 3, BLK, BLK), bf),
        ),
        in_specs=[smem] * 2 + [vmem] * 2 + [pl.BlockSpec(memory_space=pl.ANY)] * 2,
        out_specs=(vmem,) * 2 + (pl.BlockSpec(memory_space=pl.ANY),) * 2,
        scratch_shapes=[
            pltpu.VMEM((2, NG, 8, 2, GR, DW), bf),
            pltpu.VMEM((12, 16 * OWN, BLK), bf),
            pltpu.VMEM((DW, 16 * OWN), bf),
            pltpu.VMEM((73, BLK, BLK), bf),
            pltpu.VMEM((73, BLK, BLK), bf),
            pltpu.VMEM((DW, CW), bf),
            pltpu.VMEM((CW, DW), bf),
            pltpu.VMEM((NP, 4, 2, SR, CW), fl),
            pltpu.VMEM((NT, 4, SR, YW), bf),
            pltpu.VMEM((NT, 2, SR, YW // 2), bf),
            pltpu.VMEM((NT, 2, SR, YW), bf),
            pltpu.VMEM((NT, 2, 2, SR, ZW // 2), bf),
            pltpu.VMEM((NT, 2, 2, SR, ZW), bf),
            pltpu.VMEM((NT, SR, ZW), bf),
            pltpu.VMEM((NS, 4, SR, YW), bf),
            pltpu.VMEM((NS, 2, SR, YW // 2), bf),
            pltpu.VMEM((NS, 2, SR, YW), bf),
            pltpu.VMEM((NS, 2, 2, SR, ZW // 2), bf),
            pltpu.VMEM((NS, 2, 2, SR, ZW), bf),
            pltpu.VMEM((NS, SR, ZW), bf),
            pltpu.VMEM((2, NC * CB, NG, 4, 2, SR, BLK), bf),
            pltpu.VMEM((NN, SR, CW), fl),
            pltpu.VMEM((2, NG, 8, 2, GR, DW), fl),
            pltpu.VMEM((NG, 8, GR, DW), fl),
            pltpu.VMEM((NG, 4, 2, GR, DW), bf),
            pltpu.VMEM((NG, 3, 2, GR, DW), bf),
            pltpu.VMEM((NG, GR, DW), bf),
            pltpu.VMEM((NG, GR, DW), bf),
            pltpu.VMEM((2, 3, BLK, BLK), bf),
            pltpu.VMEM((2, 6, BLK, BLK), bf),
            pltpu.SMEM((12, 24), jnp.int32),
            pltpu.SMEM((24, 12), jnp.int32),
            dma((6,)),
            dma((NT, 6)), dma((NR, 6)), dma((NT, 10)), dma((NR, 10)),
            dma((2, NG, 2)), dma((2, NG, 8)), dma((NG, 3)), dma((NG, 8)),
        ],
        compiler_params=pltpu.CompilerParams(
            collective_id=1, has_side_effects=True, vmem_limit_bytes=62 * 2**20
        ),
        name="sparse_ffn",
    )(first_blocks.T, second_blocks.T, inputs, cotangent, v1, v2)
    anywhere = pl.BlockSpec(memory_space=pl.ANY)
    return pl.pallas_call(
        hand_over,
        out_shape=tuple(jax.ShapeDtypeStruct(r.shape, r.dtype) for r in results),
        in_specs=[anywhere] * 4,
        out_specs=(anywhere,) * 4,
        scratch_shapes=[pltpu.VMEM(r.shape, r.dtype) for r in results] + [dma((14,)), dma((14,))],
        name="hand_over",
    )(*results)


def solution(mesh):
    placed = (
        P("row", "col"),
        P("col", "row", None, None),
        P("col", "row"),
        P("row", "col", None, None),
        P("row", "col"),
        P("row", "col"),
    )
    return jax.shard_map(
        shards,
        mesh=mesh,
        in_specs=placed,
        out_specs=(
            P("row", "col"),
            P("row", "col"),
            P("col", "row", None, None),
            P("row", "col", None, None),
        ),
        check_vma=False,
    )
```
